32 devices in a mesh: seq: 8 (over z, x), tp: 4 (over y, core).
Axes of the slice: x: 2, y: 2, z: 4, core: 2. Of those that a mesh axis runs over, the one named last changes fastest.
Arguments:
- hidden_in: bfloat16 [2048, 1536], P('seq', 'tp'), may hold values from -6 to 6
- w_in_gate: float32 [1536, 3072], P('seq', 'tp'), may hold values from -0.15625 to 0.15625
- w_in_value: float32 [1536, 3072], P('seq', 'tp'), may hold values from -0.15625 to 0.15625
- w_in_shared: float32 [1536, 256], P('seq'), may hold values from -0.15625 to 0.15625
- w_in_step: float32 [1536, 48], P('seq', 'tp'), may hold values from -0.15625 to 0.15625
- conv_value: float32 [4, 3072], P(None, 'tp'), may hold values from -3 to 3
- conv_shared: float32 [4, 256], replicated, may hold values from -3 to 3
- dt_bias: float32 [48], P('tp'), may hold values from -4 to -2
- a_log: float32 [48], P('tp'), may hold values from -8 to 0
- skip_gain: float32 [48], P('tp'), may hold values from 0.6 to 4.8
- norm_gain: float32 [3072], P('tp'), may hold values from 0.1 to 1.9
- w_out: float32 [3072, 1536], P('tp', 'seq'), may hold values from -0.109375 to 0.109375
- prompt_lengths: int32 [8], replicated, may hold values from 1 to 1024, 2048 in all
- row_blocks: int32 [8], replicated, may hold values from 0 to 7, each once
Outputs:
- mixed_out: bfloat16 [2048, 1536], P('seq', 'tp')
The draws below stay inside these ranges and needn't reach their ends.
Inputs may be any that keep to these rules, and one draw needn't show every extreme that they name: `prompt_lengths`: 8 lengths that sum to 2048, the longest exactly 1024. `row_blocks`: a permutation of the row blocks.
All inputs are finite; a program needn't handle non-finite values.
Results may differ from the reference program's by a relative error of at most 0.02.
Values may be sent and summed in bfloat16 or wider, within the bound.
A program may use at most 128 MiB of HBM per device.

```python
import math
import jax
import jax.numpy as jnp
import numpy as np
from jax import lax

D = 1536
HEADS = 48
HEADDIM = 64
STATE = 128
KCONV = 4
SPAN = 256
PROMPTS = 8
INNER = 3072
TOKENS = 2048
MOST = 1024
ROW_BLOCKS = 8


def draw_a_log(key, part):
    first_key, second_key, third_key = jax.random.split(key, 3)
    quick_heads = jax.random.uniform(first_key, (HEADS,)) < 0.5
    quick_rate = jnp.log(jax.random.uniform(second_key, (HEADS,), minval=0.3, maxval=0.8))
    slow_rate = jnp.log(jax.random.uniform(third_key, (HEADS,), minval=12.0, maxval=40.0) / MOST)
    return jnp.where(quick_heads, quick_rate, slow_rate).astype(jnp.float32)


def draw_skip_gain(key, part):
    rising = 1.0 + 2.0 * jnp.arange(HEADS, dtype=jnp.float32) / (HEADS - 1)
    spread = jax.random.uniform(key, (HEADS,), minval=0.8, maxval=1.25)
    return (rising * spread).astype(jnp.float32)


def block_scale(stream_key, extent, cuts, low, high):
    factor_of = 1.0
    for axis_at, parts in cuts:
        steps = jax.random.uniform(jax.random.fold_in(jax.random.fold_in(stream_key, 6), axis_at), (parts,), jnp.float32, low / len(cuts), high / len(cuts))
        factor_of = factor_of * jnp.repeat(jnp.exp(steps), extent[axis_at] // parts).reshape((-1,) + (1,) * (len(extent) - 1 - axis_at))
    return factor_of


def length_profile(amount, total, limit, slope):
    loads = [(1 << 20) // math.isqrt(grade ** slope) + 1 for grade in range(2, amount + 1)]
    surplus, holding = total - limit - (amount - 1), [1] * (amount - 1)
    while surplus > 0:
        candidates = [i for i in range(amount - 1) if holding[i] < limit]
        mass, left = sum([loads[i] for i in candidates]), surplus
        for i in candidates:
            extra = min(limit - holding[i], max(1, left * loads[i] // mass), surplus)
            holding[i] = holding[i] + extra
            surplus = surplus - extra
    return np.array([limit] + holding)


def ragged(key, count, total, most, slope):
    if count == 2:
        one = jax.random.randint(key, (), max(1, total - most), min(most, total - 1) + 1)
        return jnp.stack([one, total - one])
    lengths = jnp.asarray(length_profile(count, total, most, slope), jnp.int32)
    twos = (count - 1) // 2
    donor, taker = lengths[1:1 + 2 * twos:2], lengths[2:2 + 2 * twos:2]
    margin = jnp.minimum(donor - 1, most - taker)
    passed = jax.random.randint(jax.random.fold_in(key, 1), (twos,), 0, 1 << 20) % (margin + 1)
    lengths = lengths.at[1:1 + 2 * twos:2].set(donor - passed).at[2:2 + 2 * twos:2].set(taker + passed)
    return lengths[jax.random.permutation(jax.random.fold_in(key, 2), count)]


def normal_values(stream_key, shape, scale, reach, cuts=(), kind=jnp.bfloat16):
    loudness = block_scale(stream_key, shape, cuts, -0.22, 0.18) if cuts else 1.0
    drawn = jax.random.normal(stream_key, shape, jnp.float32) * scale * loudness
    return jnp.minimum(jnp.maximum(drawn, -reach), reach).astype(kind)


def setup_inputs(seed: int = 0) -> dict:
    splits = jax.random.split(jax.random.key(seed), 15)
    return {
        "hidden_in": normal_values(splits[0], (TOKENS, D), 1.0, 6.0, ((0, 8), (1, 4))),
        "w_in_gate": normal_values(splits[1], (D, INNER), D ** -0.5, 0.15625, ((0, 8), (1, 4)), jnp.float32),
        "w_in_value": normal_values(splits[2], (D, INNER), D ** -0.5, 0.15625, ((0, 8), (1, 4)), jnp.float32),
        "w_in_shared": normal_values(splits[3], (D, 2 * STATE), D ** -0.5, 0.15625, ((0, 8),), jnp.float32),
        "w_in_step": normal_values(splits[4], (D, HEADS), D ** -0.5, 0.15625, ((0, 8), (1, 4)), jnp.float32),
        "conv_value": normal_values(splits[5], (KCONV, INNER), 0.5, 3.0, ((1, 4),), jnp.float32),
        "conv_shared": normal_values(splits[6], (KCONV, 2 * STATE), 0.5, 3.0, (), jnp.float32),
        "dt_bias": jnp.clip(-4.0 + 2.0 * jax.random.uniform(splits[7], (HEADS,), jnp.float32) ** block_scale(splits[7], (HEADS,), ((0, 4),), -0.2, 0.2), -4.0, -2.0),
        "a_log": draw_a_log(jax.random.fold_in(splits[14], 71), 0),
        "skip_gain": draw_skip_gain(jax.random.fold_in(splits[14], 71), 0),
        "norm_gain": jnp.clip(1.0 + 0.18 * jax.random.normal(splits[10], (INNER,), jnp.float32), 0.1, 1.9),
        "w_out": normal_values(splits[11], (INNER, D), INNER ** -0.5, 0.109375, ((0, 4), (1, 8)), jnp.float32),
        "prompt_lengths": ragged(splits[12], PROMPTS, TOKENS, MOST, 2).astype(jnp.int32),
        "row_blocks": jax.random.permutation(splits[13], ROW_BLOCKS).astype(jnp.int32),
    }


EPSILON = 1e-05
HIGHEST_PREC = lax.Precision.HIGHEST

def segment_of(positions, doc_ends):
    return lax.optimization_barrier(jnp.sum((positions[:, None] >= doc_ends[None, :]).astype(jnp.int32), axis=1))

def span_parts(values, b_half, c_half, steps_dt, decay_rates, segments, prev_seg):
    length = values.shape[0]
    b_rows = b_half.astype(jnp.float32)
    cumulative = jnp.cumsum(-steps_dt * decay_rates[None, :], axis=0)
    places = jnp.arange(length)
    causal = (places[:, None] >= places[None, :]) & (segments[:, None] == segments[None, :])
    gaps_log = jnp.where(causal[:, :, None], cumulative[:, None, :] - cumulative[None, :, :], 0.0)
    decays_in = jnp.where(causal[:, :, None], jnp.exp(gaps_log), 0.0)
    scores = jnp.dot(c_half, b_half.T, preferred_element_type=jnp.float32)
    weights = scores[:, :, None] * decays_in * steps_dt[None, :, :]
    intra_part = jnp.einsum('ijh,jhp->ihp', weights, values, precision=HIGHEST_PREC)
    carry_in = jnp.where((segments == prev_seg)[:, None], jnp.exp(cumulative), 0.0)
    tail_weight = jnp.where((segments == segments[-1])[:, None], jnp.exp(cumulative[-1][None, :] - cumulative), 0.0) * steps_dt
    fresh_state = jnp.einsum('jh,jhp,jn->hpn', tail_weight, values, b_rows, precision=HIGHEST_PREC)
    keep_factor = jnp.where(segments[-1] == prev_seg, jnp.exp(cumulative[-1]), 0.0)
    return (intra_part, carry_in, fresh_state, keep_factor)

def reference(hidden_in, w_in_gate, w_in_value, w_in_shared, w_in_step, conv_value, conv_shared, dt_bias, a_log, skip_gain, norm_gain, w_out, prompt_lengths, row_blocks):
    inverse_order = jnp.argsort(row_blocks).astype(jnp.int32)

    def model_rows(stored):
        blocks = stored.reshape(ROW_BLOCKS, D // ROW_BLOCKS, stored.shape[1])
        return jnp.take(blocks, inverse_order, axis=0).reshape(D, stored.shape[1]).astype(jnp.bfloat16)
    w_all = jnp.concatenate([model_rows(matrix) for matrix in (w_in_gate, w_in_value, w_in_shared, w_in_step)], axis=1)
    kernel = jnp.concatenate([conv_value, conv_shared], axis=1)
    doc_ends = jnp.cumsum(prompt_lengths).astype(jnp.int32)
    decay_rates = jnp.exp(a_log)
    out_weight = w_out.astype(jnp.bfloat16)
    span_count = TOKENS // SPAN
    edge_count = KCONV - 1
    mix_width = INNER + 2 * STATE

    def one_block(carried, inputs):
        state_in, edge_rows = carried
        block_index, block_rows = inputs
        first_pos = block_index * SPAN
        positions = first_pos + jnp.arange(SPAN, dtype=jnp.int32)
        projected = jnp.dot(block_rows, w_all, preferred_element_type=jnp.float32).astype(jnp.bfloat16)
        gate_rows = projected[:, :INNER]
        mixed_in = projected[:, INNER:INNER + mix_width]
        raw_step = projected[:, INNER + mix_width:]
        segments = segment_of(positions, doc_ends)
        edge_positions = first_pos - edge_count + jnp.arange(edge_count, dtype=jnp.int32)
        ext_segments = jnp.concatenate([segment_of(edge_positions, doc_ends), segments])
        ext_rows = jnp.concatenate([edge_rows, mixed_in], axis=0)
        conv_sum = jnp.zeros((SPAN, mix_width), jnp.float32)
        for tap_index in range(KCONV):
            same_doc = (ext_segments[tap_index:tap_index + SPAN] == segments)[:, None]
            conv_sum = conv_sum + jnp.where(same_doc, kernel[tap_index][None, :] * ext_rows[tap_index:tap_index + SPAN].astype(jnp.float32), 0.0)
        convolved = jax.nn.silu(conv_sum).astype(jnp.bfloat16)
        values = convolved[:, :INNER].astype(jnp.float32).reshape(SPAN, HEADS, HEADDIM)
        b_half = convolved[:, INNER:INNER + STATE]
        c_half = convolved[:, INNER + STATE:]
        c_rows = c_half.astype(jnp.float32)
        steps_dt = jax.nn.softplus(raw_step.astype(jnp.float32) + dt_bias[None, :])
        prev_seg = segment_of(positions[:1] - 1, doc_ends)[0]
        intra_part, carry_in, fresh_state, keep_factor = span_parts(values, b_half, c_half, steps_dt, decay_rates, segments, prev_seg)
        inter_part = jnp.einsum('in,hpn->ihp', c_rows, state_in, precision=HIGHEST_PREC) * carry_in[:, :, None]
        outputs = intra_part + inter_part + skip_gain[None, :, None] * values
        gated = outputs.reshape(SPAN, INNER) * jax.nn.silu(gate_rows.astype(jnp.float32))
        mean_square = lax.optimization_barrier(jnp.sum(gated * gated, axis=1)) / INNER
        normed = (gated * lax.rsqrt(mean_square + EPSILON)[:, None] * norm_gain[None, :]).astype(jnp.bfloat16)
        out_rows = jnp.dot(normed, out_weight, preferred_element_type=jnp.float32).astype(jnp.bfloat16)
        state_out = keep_factor[:, None, None] * state_in + fresh_state
        return ((state_out, mixed_in[SPAN - edge_count:]), out_rows)
    initial = (jnp.zeros((HEADS, HEADDIM, STATE), jnp.float32), jnp.zeros((edge_count, mix_width), jnp.bfloat16))
    blocks_in = (jnp.arange(span_count, dtype=jnp.int32), hidden_in.reshape(span_count, SPAN, D))
    last_carry, outputs = lax.scan(one_block, initial, blocks_in)
    return outputs.reshape(TOKENS, D)
```

```python
import functools

import jax
import jax.numpy as jnp
from jax import lax
from jax.experimental import pallas as pl
from jax.experimental.pallas import tpu as pltpu
from jax.sharding import PartitionSpec as P

MESH = pl.DeviceIdType.MESH
ROWS_AT_ONCE = 48

EPSILON = 1e-05
HIGHEST_PREC = lax.Precision.HIGHEST


def passed_along(block, axis, distance):
    devices = range(lax.axis_size(axis))
    route = [(i - distance, i) for i in devices if i - distance in devices]
    return lax.ppermute(block, axis, route)


def prefix_2(x, axis, combine, identity):
    count, here = (lax.axis_size(axis), lax.axis_index(axis))
    everything = jax.tree.map(
        lambda part, kind: lax.all_gather(part.astype(kind), axis), x, (jnp.bfloat16, jnp.bfloat16)
    )
    start = jax.tree.map(
        lambda part, zero: jnp.broadcast_to(jnp.asarray(zero, part.dtype), part.shape), x, identity
    )

    def turn(k, before):
        reached = k < here
        new = combine(
            before, jax.tree.map(lambda part, own: part[k].astype(own.dtype), everything, x)
        )
        return jax.tree.map(lambda a, b: jnp.where(reached, a, b), new, before)

    return lax.fori_loop(0, count, turn, start)


def segment_of(positions, doc_ends):
    return jnp.sum((positions[:, None] >= doc_ends[None, :]).astype(jnp.int32), axis=1)


def span_parts(values, b_half, c_half, steps_dt, decay_rates, segments, prev_seg):
    length = values.shape[0]
    b_rows = b_half.astype(jnp.float32)
    cumulative = jnp.cumsum(-steps_dt * decay_rates[None, :], axis=0)
    places = jnp.arange(length)
    causal = (places[:, None] >= places[None, :]) & (segments[:, None] == segments[None, :])
    gaps_log = jnp.where(causal[:, :, None], cumulative[:, None, :] - cumulative[None, :, :], 0.0)
    decays_in = jnp.where(causal[:, :, None], jnp.exp(gaps_log), 0.0)
    scores = jnp.dot(c_half, b_half.T, preferred_element_type=jnp.float32)
    weights = scores[:, :, None] * decays_in * steps_dt[None, :, :]
    intra_part = jnp.einsum("ijh,jhp->ihp", weights, values, precision=HIGHEST_PREC)
    carry_in = jnp.where((segments == prev_seg)[:, None], jnp.exp(cumulative), 0.0)
    tail_weight = (
        jnp.where(
            (segments == segments[-1])[:, None], jnp.exp(cumulative[-1][None, :] - cumulative), 0.0
        )
        * steps_dt
    )
    fresh_state = jnp.einsum("jh,jhp,jn->hpn", tail_weight, values, b_rows, precision=HIGHEST_PREC)
    keep_factor = jnp.where(segments[-1] == prev_seg, jnp.exp(cumulative[-1]), 0.0)
    return (intra_part, carry_in, fresh_state, keep_factor)


def combine(earlier, later):
    return (earlier[0] * later[0], later[0][:, None, None] * earlier[1] + later[1])


def on_device_plain(
    hidden_in,
    w_in_gate,
    w_in_value,
    w_in_shared,
    w_in_step,
    conv_value,
    conv_shared,
    dt_bias,
    a_log,
    skip_gain,
    norm_gain,
    w_out,
    prompt_lengths,
    row_blocks,
):
    seq_count = lax.axis_size("seq")
    tokens_here = hidden_in.shape[0]
    edge_count = conv_value.shape[0] - 1
    gathered = lax.all_gather(hidden_in, "tp", axis=1, tiled=True)
    row_count = gathered.shape[0]
    model_width = gathered.shape[1]
    permuted = jnp.take(
        gathered.reshape(row_count, seq_count, model_width // seq_count), row_blocks, axis=1
    ).reshape(row_count, model_width)
    stored = (
        w_in_gate.astype(jnp.bfloat16),
        w_in_value.astype(jnp.bfloat16),
        w_in_shared.astype(jnp.bfloat16),
        w_in_step.astype(jnp.bfloat16),
    )
    pieces = (
        lax.all_gather(stored[0], "seq", axis=0, tiled=True),
        lax.all_gather(stored[1], "seq", axis=0, tiled=True),
        lax.all_gather(stored[2], "seq", axis=0, tiled=True),
        lax.all_gather(stored[3], "seq", axis=0, tiled=True),
    )
    projected = tuple(
        (
            jnp.dot(permuted, weight_piece, preferred_element_type=jnp.float32)
            for weight_piece in pieces
        )
    )
    gate_all, value_all, shared_all, raw_all = [result.astype(jnp.bfloat16) for result in projected]
    mixed_in = jnp.concatenate([value_all, shared_all], axis=1)
    edge_mix = passed_along(mixed_in[tokens_here - edge_count :], "seq", 1)
    doc_ends = jnp.cumsum(prompt_lengths)
    first_pos = lax.axis_index("seq") * tokens_here
    positions = first_pos + jnp.arange(tokens_here, dtype=jnp.int32)
    edge_positions = first_pos - edge_count + jnp.arange(edge_count, dtype=jnp.int32)
    segments = segment_of(positions, doc_ends)
    ext_segments = jnp.concatenate([segment_of(edge_positions, doc_ends), segments])
    ext_rows = jnp.concatenate([edge_mix, mixed_in], axis=0)
    kernel = jnp.concatenate([conv_value, conv_shared], axis=1)
    conv_sum = jnp.zeros(mixed_in.shape, jnp.float32)
    for tap_index in range(edge_count + 1):
        same_doc = (ext_segments[tap_index : tap_index + tokens_here] == segments)[:, None]
        conv_sum = conv_sum + jnp.where(
            same_doc,
            kernel[tap_index][None, :]
            * ext_rows[tap_index : tap_index + tokens_here].astype(jnp.float32),
            0.0,
        )
    convolved = jax.nn.silu(conv_sum).astype(jnp.bfloat16)
    local_inner = conv_value.shape[1]
    local_heads = dt_bias.shape[0]
    head_dim = local_inner // local_heads
    state_size = conv_shared.shape[1] // 2
    values = (
        convolved[:, :local_inner].astype(jnp.float32).reshape(tokens_here, local_heads, head_dim)
    )
    b_half = convolved[:, local_inner : local_inner + state_size]
    c_half = convolved[:, local_inner + state_size :]
    c_rows = c_half.astype(jnp.float32)
    steps_dt = jax.nn.softplus(raw_all.astype(jnp.float32) + dt_bias[None, :])
    decay_rates = jnp.exp(a_log)
    prev_first = segment_of(jnp.reshape(first_pos - 1, (1,)), doc_ends)[0]
    device_keep = jnp.ones((local_heads,), jnp.float32)
    device_state = jnp.zeros((local_heads, head_dim, state_size), jnp.float32)
    parts = span_parts(values, b_half, c_half, steps_dt, decay_rates, segments, prev_first)
    device_keep = parts[3] * device_keep
    device_state = parts[3][:, None, None] * device_state + parts[2]
    identity = (jnp.ones_like(device_keep), jnp.zeros_like(device_state))
    prefix = prefix_2((device_keep, device_state), "seq", combine, identity)
    carried = prefix[1]
    intra_part, carry_in, fresh_state, keep_factor = parts
    inter_part = (
        jnp.einsum("in,hpn->ihp", c_rows, carried, precision=HIGHEST_PREC) * carry_in[:, :, None]
    )
    outputs = intra_part + inter_part
    mixed_heads = outputs + skip_gain[None, :, None] * values
    gated = mixed_heads.reshape(tokens_here, local_inner) * jax.nn.silu(
        gate_all.astype(jnp.float32)
    )
    squares = jnp.sum(gated * gated, axis=1)
    square_total = lax.psum(squares, "tp")
    mean_square = square_total / (local_inner * lax.axis_size("tp"))
    normed = (gated * lax.rsqrt(mean_square + EPSILON)[:, None] * norm_gain[None, :]).astype(
        jnp.bfloat16
    )
    out_weight = w_out.astype(jnp.bfloat16)
    partial_terms = jnp.dot(
        normed,
        lax.all_gather(out_weight, "seq", axis=1, tiled=True),
        preferred_element_type=jnp.float32,
    )
    return lax.psum_scatter(
        partial_terms.astype(jnp.bfloat16), "tp", scatter_dimension=1, tiled=True
    )


def place():
    seq, tp = lax.axis_index("seq"), lax.axis_index("tp")
    return seq, tp, seq // 2, seq % 2, tp // 2, tp % 2


def remote(src, dst, send, recv, seq, tp):
    return pltpu.make_async_remote_copy(
        src_ref=src, dst_ref=dst, send_sem=send, recv_sem=recv,
        device_id=(seq, tp), device_id_type=MESH,
    )


def greet_plane(planes):
    seq, tp, z, x, y, c = place()
    barrier = pltpu.get_barrier_semaphore()
    for other in range(1, 8):
        dx, dt = other // 4, other % 4
        pl.semaphore_signal(
            barrier, inc=1, device_id=(2 * z + (x + dx) % 2, (tp + dt) % 4), device_id_type=MESH
        )

    if planes > 1:
        @pl.when(z > 0)
        def _():
            pl.semaphore_signal(barrier, inc=1, device_id=(seq - 2, tp), device_id_type=MESH)

        @pl.when(z < planes - 1)
        def _():
            pl.semaphore_signal(barrier, inc=1, device_id=(seq + 2, tp), device_id_type=MESH)

    extra = (0 if planes == 1 else 1) + jnp.where((z > 0) & (z < planes - 1), 1, 0)
    pl.semaphore_wait(barrier, 7 + extra)


def gather_kernel(
    planes, h_ref, w_ref, p_ref, hid_ref, all_ref, par_ref,
    got, swapped, up, down, across, h_send, h_got, p_sems,
):
    seq, tp, z, x, y, c = place()
    chunks = w_ref.shape[0] // ROWS_AT_ONCE
    mine = 2 * z + c
    greet_plane(planes)

    def rows(k):
        return pl.ds(pl.multiple_of(k * ROWS_AT_ONCE, ROWS_AT_ONCE), ROWS_AT_ONCE)

    def local_part(k):
        return pltpu.make_async_copy(w_ref.at[rows(k)], all_ref.at[mine, rows(k)], got.at[mine, k])

    def swap_part(k):
        slot = 2 * z + 1 - c
        return remote(
            w_ref.at[rows(k)], all_ref.at[slot, rows(k)], swapped.at[k], got.at[slot, k],
            seq + 1 - 2 * x, tp + 1 - 2 * c,
        )

    def landed(slot, k):
        here = all_ref.at[slot, rows(k)]
        return remote(here, here, swapped.at[k], got.at[slot, k], seq, tp + 1 - 2 * c)

    def sent(slot, k, sems, to_seq, to_tp):
        here = all_ref.at[slot, rows(k)]
        return remote(here, here, sems.at[slot // 2, k], got.at[slot, k], to_seq, to_tp)

    par_local = pltpu.make_async_copy(p_ref, par_ref, p_sems.at[0])
    par_swap = remote(p_ref, par_ref, p_sems.at[1], p_sems.at[0], seq + 1 - 2 * x, tp + 1 - 2 * c)

    @pl.when(x == c)
    def _():
        @pl.loop(0, chunks)
        def _(k):
            local_part(k).start()
        par_local.start()

    @pl.when(x != c)
    def _():
        @pl.loop(0, chunks)
        def _(k):
            swap_part(k).start()
        par_swap.start()

    def features(to):
        return remote(
            h_ref, hid_ref.at[tp], h_send.at[to], h_got.at[tp], 2 * z + to // 2, 2 * (to % 2) + x
        )

    own_features = pltpu.make_async_copy(h_ref, hid_ref.at[tp], h_got.at[tp])
    for to in range(4):
        itself = (x == c) & (x == to // 2) & (y == to % 2)

        @pl.when(itself)
        def _():
            own_features.start()

        @pl.when(jnp.logical_not(itself))
        def _():
            features(to).start()

    def hand_on(slot, k, going_up, going_down):
        if going_up:
            @pl.when(z < planes - 1)
            def _():
                sent(slot, k, up, seq + 2, tp).start()
        if going_down:
            @pl.when(z > 0)
            def _():
                sent(slot, k, down, seq - 2, tp).start()
        sent(slot, k, across, seq, tp + 1 - 2 * c).start()

    @pl.loop(0, chunks)
    def _(k):
        @pl.when(x == c)
        def _():
            local_part(k).wait()

        @pl.when(x != c)
        def _():
            landed(mine, k).wait_recv()

        hand_on(mine, k, True, True)

    for far in range(1, planes):
        @pl.loop(0, chunks)
        def _(k):
            @pl.when(z >= far)
            def _():
                landed(mine - 2 * far, k).wait_recv()
                hand_on(mine - 2 * far, k, True, False)

            @pl.when(z < planes - far)
            def _():
                landed(mine + 2 * far, k).wait_recv()
                hand_on(mine + 2 * far, k, False, True)

    @pl.loop(0, chunks)
    def _(k):
        for at in range(planes):
            slot = 2 * at + c
            landed(2 * at + 1 - c, k).wait_recv()
            sent(slot, k, across, seq, tp + 1 - 2 * c).wait_send()

            @pl.when((z < planes - 1) & (z >= at))
            def _():
                sent(slot, k, up, seq + 2, tp).wait_send()

            @pl.when((z > 0) & (z <= at))
            def _():
                sent(slot, k, down, seq - 2, tp).wait_send()

        @pl.when(x != c)
        def _():
            swap_part(k).wait_send()

    for to in range(4):
        itself = (x == c) & (x == to // 2) & (y == to % 2)

        @pl.when(jnp.logical_not(itself))
        def _():
            features(to).wait_send()

    for quarter in range(4):
        remote(
            h_ref, hid_ref.at[quarter], h_send.at[0], h_got.at[quarter], seq, tp + 1 - 2 * c
        ).wait_recv()

    @pl.when(x == c)
    def _():
        par_local.wait()

    @pl.when(x != c)
    def _():
        par_swap.wait()


def gather_all(hidden, packed, params, planes):
    any_spec = pl.BlockSpec(memory_space=pl.ANY)
    blocks, chunks = 2 * planes, packed.shape[0] // ROWS_AT_ONCE
    dma = pltpu.SemaphoreType.DMA
    return pl.pallas_call(
        functools.partial(gather_kernel, planes),
        out_shape=(
            jax.ShapeDtypeStruct((4,) + hidden.shape, hidden.dtype),
            jax.ShapeDtypeStruct((blocks,) + packed.shape, packed.dtype),
            jax.ShapeDtypeStruct(params.shape, params.dtype),
        ),
        in_specs=[any_spec] * 3,
        out_specs=[any_spec] * 3,
        scratch_shapes=[
            dma((blocks, chunks)), dma((chunks,)), dma((planes, chunks)), dma((planes, chunks)),
            dma((planes, chunks)), dma((4,)), dma((4,)), dma((2,)),
        ],
        compiler_params=pltpu.CompilerParams(collective_id=0, has_side_effects=True),
        name="gather_weights",
    )(hidden, packed, params)


def chain_kernel(planes, fresh_ref, keep_ref, state_ref, arrived, leaving, send, recv):
    seq, tp, z, x, y, c = place()
    first, last = (z == 0) & (c == 0), (z == planes - 1) & (c == 1)
    before = (seq - 2 * (1 - c), tp + 1 - 2 * c)
    after = (seq + 2 * c, tp + 1 - 2 * c)
    barrier = pltpu.get_barrier_semaphore()

    @pl.when(jnp.logical_not(first))
    def _():
        pl.semaphore_signal(barrier, inc=1, device_id=before, device_id_type=MESH)

    @pl.when(jnp.logical_not(last))
    def _():
        pl.semaphore_signal(barrier, inc=1, device_id=after, device_id_type=MESH)

    pl.semaphore_wait(barrier, jnp.where(first | last, 1, 2))
    half = fresh_ref.shape[0] // 2
    for part in range(2):
        heads = pl.ds(part * half, half)

        def onward():
            return remote(
                leaving.at[heads], arrived.at[heads], send.at[part], recv.at[part], *after
            )

        @pl.when(first)
        def _():
            state_ref[heads] = jnp.zeros((half,) + state_ref.shape[1:], jnp.float32)

        @pl.when(jnp.logical_not(first))
        def _():
            remote(
                leaving.at[heads], arrived.at[heads], send.at[part], recv.at[part], *before
            ).wait_recv()
            state_ref[heads] = arrived[heads].astype(jnp.float32)

        @pl.when(jnp.logical_not(last))
        def _():
            leaving[heads] = (keep_ref[heads] * state_ref[heads] + fresh_ref[heads]).astype(
                jnp.bfloat16
            )
            onward().start()

    for part in range(2):
        heads = pl.ds(part * half, half)

        @pl.when(jnp.logical_not(last))
        def _():
            remote(
                leaving.at[heads], arrived.at[heads], send.at[part], recv.at[part], *after
            ).wait_send()


def chain_states(fresh, keep, planes):
    keep_rows = jnp.broadcast_to(keep[:, None, None], (keep.shape[0], 1, fresh.shape[2]))
    dma = pltpu.SemaphoreType.DMA
    return pl.pallas_call(
        functools.partial(chain_kernel, planes),
        out_shape=jax.ShapeDtypeStruct(fresh.shape, jnp.float32),
        in_specs=[pl.BlockSpec(memory_space=pltpu.VMEM)] * 2,
        out_specs=pl.BlockSpec(memory_space=pltpu.VMEM),
        scratch_shapes=[
            pltpu.VMEM(fresh.shape, jnp.bfloat16), pltpu.VMEM(fresh.shape, jnp.bfloat16),
            dma((2,)), dma((2,)),
        ],
        compiler_params=pltpu.CompilerParams(
            collective_id=1, has_side_effects=True, vmem_limit_bytes=16 << 20
        ),
        name="chain_states",
    )(fresh, keep_rows)


def tail_kernel(
    inner_total, start, gated_ref, gain_ref, all_ref, out_ref,
    weight, leaving, arrived, sq_leaving, sq_arrived, load, send, recv, sq_send, sq_recv,
):
    seq, tp, z, x, y, c = place()
    share = 2 * y + x
    width = gated_ref.shape[1]
    fetch = pltpu.make_async_copy(all_ref.at[:, :, pl.ds(start, width)], weight, load.at[0])
    fetch.start()
    greet_plane(1)
    gated = gated_ref[...]
    sums = lax.dot_general(
        jnp.ones((8, width), jnp.float32), gated * gated, (((1,), (1,)), ((), ())),
        precision=HIGHEST_PREC, preferred_element_type=jnp.float32,
    )
    sq_leaving[...] = sums
    scaled = (gated * gain_ref[...]).astype(jnp.bfloat16)
    fetch.wait()
    columns = 2 * weight.shape[1]

    def outward(to):
        return remote(leaving.at[to], arrived.at[share], send.at[to], recv.at[share], 2 * z + c, to)

    def squares(to):
        return remote(
            sq_leaving, sq_arrived.at[share], sq_send.at[to], sq_recv.at[share], 2 * z + c, to
        )

    for to in range(4):
        block = weight[2 * to : 2 * to + 2].reshape(columns, width)
        product = lax.dot_general(
            scaled, block, (((1,), (1,)), ((), ())), preferred_element_type=jnp.float32
        ).astype(jnp.bfloat16)
        itself = (x == c) & (tp == to)

        @pl.when(itself)
        def _():
            arrived[share] = product
            sq_arrived[share] = sums

        @pl.when(jnp.logical_not(itself))
        def _():
            leaving[to] = product
            outward(to).start()
            squares(to).start()

    total, sq_total = 0.0, 0.0
    for slot in range(4):
        @pl.when(jnp.logical_not((x == c) & (share == slot)))
        def _():
            remote(
                leaving.at[0], arrived.at[slot], send.at[0], recv.at[slot], seq, tp + 1 - 2 * c
            ).wait_recv()
            remote(
                sq_leaving, sq_arrived.at[slot], sq_send.at[0], sq_recv.at[slot],
                seq, tp + 1 - 2 * c,
            ).wait_recv()

        total = total + arrived[slot].astype(jnp.float32)
        sq_total = sq_total + sq_arrived[slot]
    scale = lax.rsqrt(sq_total[0:1] / inner_total + EPSILON)
    scale_rows = jnp.transpose(jnp.broadcast_to(scale, (128, scale.shape[1])))[:, 0:1]
    out_ref[...] = (total * scale_rows).astype(out_ref.dtype)

    for to in range(4):
        itself = (x == c) & (tp == to)

        @pl.when(jnp.logical_not(itself))
        def _():
            outward(to).wait_send()
            squares(to).wait_send()


def finish(gated, gain, gathered, start, width_here, inner_total):
    rows, width = gated.shape
    blocks, depth = gathered.shape[:2]
    dma = pltpu.SemaphoreType.DMA
    return pl.pallas_call(
        functools.partial(tail_kernel, inner_total, start),
        out_shape=jax.ShapeDtypeStruct((rows, width_here), jnp.bfloat16),
        in_specs=[
            pl.BlockSpec(memory_space=pltpu.VMEM),
            pl.BlockSpec(memory_space=pltpu.VMEM),
            pl.BlockSpec(memory_space=pl.ANY),
        ],
        out_specs=pl.BlockSpec(memory_space=pltpu.VMEM),
        scratch_shapes=[
            pltpu.VMEM((blocks, depth, width), jnp.bfloat16),
            pltpu.VMEM((4, rows, width_here), jnp.bfloat16),
            pltpu.VMEM((4, rows, width_here), jnp.bfloat16),
            pltpu.VMEM((8, rows), jnp.float32),
            pltpu.VMEM((4, 8, rows), jnp.float32),
            dma((1,)), dma((4,)), dma((4,)), dma((4,)), dma((4,)),
        ],
        compiler_params=pltpu.CompilerParams(
            collective_id=2, has_side_effects=True, vmem_limit_bytes=32 << 20
        ),
        name="project_out",
    )(gated, gain, gathered)


def on_device_paired(
    hidden_in,
    w_in_gate,
    w_in_value,
    w_in_shared,
    w_in_step,
    conv_value,
    conv_shared,
    dt_bias,
    a_log,
    skip_gain,
    norm_gain,
    w_out,
    prompt_lengths,
    row_blocks,
):
    seq_count = lax.axis_size("seq")
    planes = seq_count // 2
    here = 2 * (lax.axis_index("seq") // 2) + lax.axis_index("tp") % 2
    tokens_here = hidden_in.shape[0]
    edge_count = conv_value.shape[0] - 1
    local_inner = conv_value.shape[1]
    local_heads = dt_bias.shape[0]
    shared_width = conv_shared.shape[1]
    head_dim = local_inner // local_heads
    state_size = shared_width // 2
    rows_here = w_in_gate.shape[0]
    step_width = 128
    packed = jnp.concatenate(
        [
            w_in_value.astype(jnp.bfloat16),
            w_in_shared.astype(jnp.bfloat16),
            w_in_gate.astype(jnp.bfloat16),
            jnp.pad(w_in_step.astype(jnp.bfloat16), ((0, 0), (0, step_width - local_heads))),
            w_out.astype(jnp.bfloat16).T,
        ],
        axis=1,
    )
    scalars = jnp.pad(
        jnp.concatenate([dt_bias, a_log, skip_gain]), (0, local_inner - 3 * local_heads)
    )
    spare = jnp.zeros((8 - edge_count - 3, local_inner), jnp.float32)
    params = jnp.concatenate([conv_value, norm_gain[None], scalars[None], spare], axis=0)
    features, gathered, params = gather_all(hidden_in, packed, params, planes)
    taps_value = params[: edge_count + 1]
    norm_gain = params[edge_count + 1]
    scalars = params[edge_count + 2]
    dt_bias = scalars[:local_heads]
    a_log = scalars[local_heads : 2 * local_heads]
    skip_gain = scalars[2 * local_heads : 3 * local_heads]

    model_width = features.shape[0] * features.shape[2]
    by_block = jnp.transpose(features, (1, 0, 2)).reshape(
        tokens_here, seq_count, model_width // seq_count
    )
    permuted = jnp.take(by_block, row_blocks, axis=1).reshape(tokens_here, model_width)
    in_width = 2 * local_inner + shared_width + step_width
    projected = jnp.dot(
        permuted,
        gathered[:, :, :in_width].reshape(model_width, in_width),
        preferred_element_type=jnp.float32,
    ).astype(jnp.bfloat16)
    mix_width = local_inner + shared_width
    mixed_in = projected[:, :mix_width]
    gate_all = projected[:, mix_width : mix_width + local_inner]
    raw_all = projected[:, mix_width + local_inner : mix_width + local_inner + local_heads]

    tp_count = lax.axis_size("tp")

    def device(block, share):
        z, c, y, x = block // 2, block % 2, share // 2, share % 2
        return (2 * z + x) * tp_count + 2 * y + c

    route = [
        (device(block, share), device(block + 1, share))
        for block in range(seq_count - 1)
        for share in range(tp_count)
    ]
    edge_mix = lax.ppermute(mixed_in[tokens_here - edge_count :], ("seq", "tp"), route)
    doc_ends = jnp.cumsum(prompt_lengths)
    first_pos = here * tokens_here
    positions = first_pos + jnp.arange(tokens_here, dtype=jnp.int32)
    edge_positions = first_pos - edge_count + jnp.arange(edge_count, dtype=jnp.int32)
    segments = segment_of(positions, doc_ends)
    ext_segments = jnp.concatenate([segment_of(edge_positions, doc_ends), segments])
    ext_rows = jnp.concatenate([edge_mix, mixed_in], axis=0)
    kernel = jnp.concatenate([taps_value, conv_shared], axis=1)
    conv_sum = jnp.zeros(mixed_in.shape, jnp.float32)
    for tap_index in range(edge_count + 1):
        same_doc = (ext_segments[tap_index : tap_index + tokens_here] == segments)[:, None]
        conv_sum = conv_sum + jnp.where(
            same_doc,
            kernel[tap_index][None, :]
            * ext_rows[tap_index : tap_index + tokens_here].astype(jnp.float32),
            0.0,
        )
    convolved = jax.nn.silu(conv_sum).astype(jnp.bfloat16)
    values = (
        convolved[:, :local_inner].astype(jnp.float32).reshape(tokens_here, local_heads, head_dim)
    )
    b_half = convolved[:, local_inner : local_inner + state_size]
    c_half = convolved[:, local_inner + state_size :]
    c_rows = c_half.astype(jnp.float32)
    steps_dt = jax.nn.softplus(raw_all.astype(jnp.float32) + dt_bias[None, :])
    decay_rates = jnp.exp(a_log)
    prev_first = segment_of(jnp.reshape(first_pos - 1, (1,)), doc_ends)[0]
    parts = span_parts(values, b_half, c_half, steps_dt, decay_rates, segments, prev_first)
    carried = chain_states(parts[2], parts[3], planes)
    intra_part, carry_in, _, _ = parts
    inter_part = (
        jnp.einsum("in,hpn->ihp", c_rows, carried, precision=HIGHEST_PREC) * carry_in[:, :, None]
    )
    outputs = intra_part + inter_part
    mixed_heads = outputs + skip_gain[None, :, None] * values
    gated = mixed_heads.reshape(tokens_here, local_inner) * jax.nn.silu(
        gate_all.astype(jnp.float32)
    )
    return finish(
        gated,
        norm_gain[None],
        gathered,
        in_width,
        hidden_in.shape[1],
        local_inner * tp_count,
    )


def paired(mesh):
    return dict(mesh.shape) == {"seq": 8, "tp": 4}


def solution(mesh):
    return jax.shard_map(
        on_device_paired if paired(mesh) else on_device_plain,
        mesh=mesh,
        in_specs=(
            P("seq", "tp"),
            P("seq", "tp"),
            P("seq", "tp"),
            P("seq", None),
            P("seq", "tp"),
            P(None, "tp"),
            P(),
            P("tp"),
            P("tp"),
            P("tp"),
            P("tp"),
            P("tp", "seq"),
            P(),
            P(),
        ),
        out_specs=P("seq", "tp"),
        check_vma=False,
    )
```

```python
import functools

import jax
import jax.numpy as jnp
from jax import lax
from jax.experimental import pallas as pl
from jax.experimental.pallas import tpu as pltpu
from jax.sharding import PartitionSpec as P

MESH = pl.DeviceIdType.MESH

EPSILON = 1e-05
HIGHEST_PREC = lax.Precision.HIGHEST


def passed_along(block, axis, distance):
    devices = range(lax.axis_size(axis))
    route = [(i - distance, i) for i in devices if i - distance in devices]
    return lax.ppermute(block, axis, route)


def prefix_2(x, axis, combine, identity):
    count, here = (lax.axis_size(axis), lax.axis_index(axis))
    everything = jax.tree.map(
        lambda part, kind: lax.all_gather(part.astype(kind), axis), x, (jnp.bfloat16, jnp.bfloat16)
    )
    start = jax.tree.map(
        lambda part, zero: jnp.broadcast_to(jnp.asarray(zero, part.dtype), part.shape), x, identity
    )

    def turn(k, before):
        reached = k < here
        new = combine(
            before, jax.tree.map(lambda part, own: part[k].astype(own.dtype), everything, x)
        )
        return jax.tree.map(lambda a, b: jnp.where(reached, a, b), new, before)

    return lax.fori_loop(0, count, turn, start)


def segment_of(positions, doc_ends):
    return jnp.sum((positions[:, None] >= doc_ends[None, :]).astype(jnp.int32), axis=1)


def span_parts(values, b_half, c_half, steps_dt, decay_rates, segments, prev_seg):
    length = values.shape[0]
    b_rows = b_half.astype(jnp.float32)
    cumulative = jnp.cumsum(-steps_dt * decay_rates[None, :], axis=0)
    places = jnp.arange(length)
    causal = (places[:, None] >= places[None, :]) & (segments[:, None] == segments[None, :])
    gaps_log = jnp.where(causal[:, :, None], cumulative[:, None, :] - cumulative[None, :, :], 0.0)
    decays_in = jnp.where(causal[:, :, None], jnp.exp(gaps_log), 0.0)
    scores = jnp.dot(c_half, b_half.T, preferred_element_type=jnp.float32)
    weights = scores[:, :, None] * decays_in * steps_dt[None, :, :]
    intra_part = jnp.einsum("ijh,jhp->ihp", weights, values, precision=HIGHEST_PREC)
    carry_in = jnp.where((segments == prev_seg)[:, None], jnp.exp(cumulative), 0.0)
    tail_weight = (
        jnp.where(
            (segments == segments[-1])[:, None], jnp.exp(cumulative[-1][None, :] - cumulative), 0.0
        )
        * steps_dt
    )
    fresh_state = jnp.einsum("jh,jhp,jn->hpn", tail_weight, values, b_rows, precision=HIGHEST_PREC)
    keep_factor = jnp.where(segments[-1] == prev_seg, jnp.exp(cumulative[-1]), 0.0)
    return (intra_part, carry_in, fresh_state, keep_factor)


def combine(earlier, later):
    return (earlier[0] * later[0], later[0][:, None, None] * earlier[1] + later[1])


def on_device_plain(
    hidden_in,
    w_in_gate,
    w_in_value,
    w_in_shared,
    w_in_step,
    conv_value,
    conv_shared,
    dt_bias,
    a_log,
    skip_gain,
    norm_gain,
    w_out,
    prompt_lengths,
    row_blocks,
):
    seq_count = lax.axis_size("seq")
    tokens_here = hidden_in.shape[0]
    edge_count = conv_value.shape[0] - 1
    gathered = lax.all_gather(hidden_in, "tp", axis=1, tiled=True)
    row_count = gathered.shape[0]
    model_width = gathered.shape[1]
    permuted = jnp.take(
        gathered.reshape(row_count, seq_count, model_width // seq_count), row_blocks, axis=1
    ).reshape(row_count, model_width)
    stored = (
        w_in_gate.astype(jnp.bfloat16),
        w_in_value.astype(jnp.bfloat16),
        w_in_shared.astype(jnp.bfloat16),
        w_in_step.astype(jnp.bfloat16),
    )
    pieces = (
        lax.all_gather(stored[0], "seq", axis=0, tiled=True),
        lax.all_gather(stored[1], "seq", axis=0, tiled=True),
        lax.all_gather(stored[2], "seq", axis=0, tiled=True),
        lax.all_gather(stored[3], "seq", axis=0, tiled=True),
    )
    projected = tuple(
        (
            jnp.dot(permuted, weight_piece, preferred_element_type=jnp.float32)
            for weight_piece in pieces
        )
    )
    gate_all, value_all, shared_all, raw_all = [result.astype(jnp.bfloat16) for result in projected]
    mixed_in = jnp.concatenate([value_all, shared_all], axis=1)
    edge_mix = passed_along(mixed_in[tokens_here - edge_count :], "seq", 1)
    doc_ends = jnp.cumsum(prompt_lengths)
    first_pos = lax.axis_index("seq") * tokens_here
    positions = first_pos + jnp.arange(tokens_here, dtype=jnp.int32)
    edge_positions = first_pos - edge_count + jnp.arange(edge_count, dtype=jnp.int32)
    segments = segment_of(positions, doc_ends)
    ext_segments = jnp.concatenate([segment_of(edge_positions, doc_ends), segments])
    ext_rows = jnp.concatenate([edge_mix, mixed_in], axis=0)
    kernel = jnp.concatenate([conv_value, conv_shared], axis=1)
    conv_sum = jnp.zeros(mixed_in.shape, jnp.float32)
    for tap_index in range(edge_count + 1):
        same_doc = (ext_segments[tap_index : tap_index + tokens_here] == segments)[:, None]
        conv_sum = conv_sum + jnp.where(
            same_doc,
            kernel[tap_index][None, :]
            * ext_rows[tap_index : tap_index + tokens_here].astype(jnp.float32),
            0.0,
        )
    convolved = jax.nn.silu(conv_sum).astype(jnp.bfloat16)
    local_inner = conv_value.shape[1]
    local_heads = dt_bias.shape[0]
    head_dim = local_inner // local_heads
    state_size = conv_shared.shape[1] // 2
    values = (
        convolved[:, :local_inner].astype(jnp.float32).reshape(tokens_here, local_heads, head_dim)
    )
    b_half = convolved[:, local_inner : local_inner + state_size]
    c_half = convolved[:, local_inner + state_size :]
    c_rows = c_half.astype(jnp.float32)
    steps_dt = jax.nn.softplus(raw_all.astype(jnp.float32) + dt_bias[None, :])
    decay_rates = jnp.exp(a_log)
    prev_first = segment_of(jnp.reshape(first_pos - 1, (1,)), doc_ends)[0]
    device_keep = jnp.ones((local_heads,), jnp.float32)
    device_state = jnp.zeros((local_heads, head_dim, state_size), jnp.float32)
    parts = span_parts(values, b_half, c_half, steps_dt, decay_rates, segments, prev_first)
    device_keep = parts[3] * device_keep
    device_state = parts[3][:, None, None] * device_state + parts[2]
    identity = (jnp.ones_like(device_keep), jnp.zeros_like(device_state))
    prefix = prefix_2((device_keep, device_state), "seq", combine, identity)
    carried = prefix[1]
    intra_part, carry_in, fresh_state, keep_factor = parts
    inter_part = (
        jnp.einsum("in,hpn->ihp", c_rows, carried, precision=HIGHEST_PREC) * carry_in[:, :, None]
    )
    outputs = intra_part + inter_part
    mixed_heads = outputs + skip_gain[None, :, None] * values
    gated = mixed_heads.reshape(tokens_here, local_inner) * jax.nn.silu(
        gate_all.astype(jnp.float32)
    )
    squares = jnp.sum(gated * gated, axis=1)
    square_total = lax.psum(squares, "tp")
    mean_square = square_total / (local_inner * lax.axis_size("tp"))
    normed = (gated * lax.rsqrt(mean_square + EPSILON)[:, None] * norm_gain[None, :]).astype(
        jnp.bfloat16
    )
    out_weight = w_out.astype(jnp.bfloat16)
    partial_terms = jnp.dot(
        normed,
        lax.all_gather(out_weight, "seq", axis=1, tiled=True),
        preferred_element_type=jnp.float32,
    )
    return lax.psum_scatter(
        partial_terms.astype(jnp.bfloat16), "tp", scatter_dimension=1, tiled=True
    )


def place():
    seq, tp = lax.axis_index("seq"), lax.axis_index("tp")
    return seq, tp, seq // 2, seq % 2, tp // 2, tp % 2


def remote(src, dst, send, recv, seq, tp):
    return pltpu.make_async_remote_copy(
        src_ref=src, dst_ref=dst, send_sem=send, recv_sem=recv,
        device_id=(seq, tp), device_id_type=MESH,
    )


def greet(planes):
    seq, tp, z, x, y, c = place()
    barrier = pltpu.get_barrier_semaphore()

    def meet(to_seq, to_tp):
        pl.semaphore_signal(barrier, inc=1, device_id=(to_seq, to_tp), device_id_type=MESH)

    for other in range(1, 8):
        dx, dt = other // 4, other % 4
        meet(2 * z + (x + dx) % 2, (tp + dt) % 4)

    @pl.when(z > 0)
    def _():
        meet(seq - 2, tp)

        @pl.when(c == 0)
        def _():
            meet(seq - 2, tp + 1)

    @pl.when(z < planes - 1)
    def _():
        meet(seq + 2, tp)

        @pl.when(c == 1)
        def _():
            meet(seq + 2, tp - 1)

    below = jnp.where(z > 0, 2 - c, 0)
    above = jnp.where(z < planes - 1, 1 + c, 0)
    pl.semaphore_wait(barrier, 7 + below + above)


class Relay:
    def __init__(self, planes, depth, own, every, sems):
        self.planes, self.depth, self.own, self.every = planes, depth, own, every
        self.got, self.swapped, self.up, self.down, self.across = sems
        self.chunks = own.shape[0] // depth
        self.at = place()

    def rows(self, k):
        return pl.ds(pl.multiple_of(k * self.depth, self.depth), self.depth)

    def local(self, k):
        seq, tp, z, x, y, c = self.at
        return pltpu.make_async_copy(
            self.own.at[self.rows(k)], self.every.at[2 * z + c, self.rows(k)], self.got.at[2 * z + c, k]
        )

    def swap(self, k):
        seq, tp, z, x, y, c = self.at
        slot = 2 * z + 1 - c
        return remote(
            self.own.at[self.rows(k)], self.every.at[slot, self.rows(k)],
            self.swapped.at[k], self.got.at[slot, k], seq + 1 - 2 * x, tp + 1 - 2 * c,
        )

    def sent(self, slot, k, sems, to_seq, to_tp):
        here = self.every.at[slot, self.rows(k)]
        return remote(here, here, sems.at[slot // 2, k], self.got.at[slot, k], to_seq, to_tp)

    def going_up(self, slot, k):
        return self.sent(slot, k, self.up, self.at[0] + 2, self.at[1])

    def going_down(self, slot, k):
        return self.sent(slot, k, self.down, self.at[0] - 2, self.at[1])

    def going_across(self, slot, k):
        return self.sent(slot, k, self.across, self.at[0], self.at[1] + 1 - 2 * self.at[5])

    def start(self):
        seq, tp, z, x, y, c = self.at

        @pl.when(x == c)
        def _():
            @pl.loop(0, self.chunks)
            def _(k):
                self.local(k).start()

        @pl.when(x != c)
        def _():
            @pl.loop(0, self.chunks)
            def _(k):
                self.swap(k).start()

    def turn(self, far):
        seq, tp, z, x, y, c = self.at
        mine = 2 * z + c

        @pl.loop(0, self.chunks)
        def _(k):
            if far == 0:
                @pl.when(x == c)
                def _():
                    self.local(k).wait()

                @pl.when(x != c)
                def _():
                    self.going_across(mine, k).wait_recv()

                @pl.when(z < self.planes - 1)
                def _():
                    self.going_up(mine, k).start()

                @pl.when(z > 0)
                def _():
                    self.going_down(mine, k).start()

                self.going_across(mine, k).start()
            else:
                @pl.when(z >= far)
                def _():
                    slot = mine - 2 * far
                    self.going_across(slot, k).wait_recv()

                    @pl.when(z < self.planes - 1)
                    def _():
                        self.going_up(slot, k).start()

                    self.going_across(slot, k).start()

                @pl.when(z < self.planes - far)
                def _():
                    slot = mine + 2 * far
                    self.going_across(slot, k).wait_recv()

                    @pl.when(z > 0)
                    def _():
                        self.going_down(slot, k).start()

                    self.going_across(slot, k).start()

    def arrive(self):
        c = self.at[5]

        @pl.loop(0, self.chunks)
        def _(k):
            for at in range(self.planes):
                self.going_across(2 * at + 1 - c, k).wait_recv()

    def leave(self):
        seq, tp, z, x, y, c = self.at

        @pl.loop(0, self.chunks)
        def _(k):
            for at in range(self.planes):
                slot = 2 * at + c
                self.going_across(slot, k).wait_send()

                @pl.when((z < self.planes - 1) & (z >= at))
                def _():
                    self.going_up(slot, k).wait_send()

                @pl.when((z > 0) & (z <= at))
                def _():
                    self.going_down(slot, k).wait_send()

            @pl.when(x != c)
            def _():
                self.swap(k).wait_send()


def mixer_kernel(
    planes, heads, inner_total,
    lengths_ref, order_ref, h_ref, gate_ref, value_ref, shared_ref, step_ref, taps_ref,
    shared_taps_ref, bias_ref, log_ref, skip_ref, gain_ref, w_out_ref, out_ref,
    w_own, w_all, o_all, h_own, h_all, p_own, par, gates, rows_ext, edge_own, edge_got, mixed,
    fresh, state_got, state_own, leaving, arrived, sq_leaving, sq_arrived,
    w_got, w_swapped, w_up, w_down, w_across, o_got, o_swapped, o_up, o_down, o_across,
    h_send, h_got, p_sems, edge_sems, state_sems, send, recv, sq_send, sq_recv,
):
    f32, bf16 = jnp.float32, jnp.bfloat16
    seq, tp, z, x, y, c = place()
    share = 2 * y + x
    first, last = (z == 0) & (c == 0), (z == planes - 1) & (c == 1)
    before = (seq - 2 * (1 - c), tp + 1 - 2 * c)
    after = (seq + 2 * c, tp + 1 - 2 * c)
    tokens, width = h_ref.shape[0], value_ref.shape[1]
    shared_width = shared_ref.shape[1]
    mix_width, state_size, head_dim = width + shared_width, shared_width // 2, width // heads
    half_features = h_ref.shape[1] // 2
    step_at = mix_width + width

    w_own[:, 0:width] = value_ref[...].astype(bf16)
    w_own[:, width:mix_width] = shared_ref[...].astype(bf16)
    w_own[:, mix_width:step_at] = gate_ref[...].astype(bf16)
    w_own[:, step_at:] = jnp.zeros((w_own.shape[0], w_own.shape[1] - step_at), bf16)
    w_own[:, step_at : step_at + heads] = step_ref[...].astype(bf16)
    h_own[0] = h_ref[:, 0:half_features]
    h_own[1] = h_ref[:, half_features:]
    p_own[...] = jnp.zeros_like(p_own)
    p_own[0:4, :] = taps_ref[...]
    p_own[4:5, :] = gain_ref[...]
    p_own[5:6, 0:heads] = bias_ref[...]
    p_own[6:7, 0:heads] = log_ref[...]
    p_own[7:8, 0:heads] = skip_ref[...]
    greet(planes)

    into = Relay(planes, 48, w_own, w_all, (w_got, w_swapped, w_up, w_down, w_across))
    out_of = Relay(planes, 96, w_out_ref, o_all, (o_got, o_swapped, o_up, o_down, o_across))
    par_local = pltpu.make_async_copy(p_own, par, p_sems.at[0])
    par_swap = remote(p_own, par, p_sems.at[1], p_sems.at[0], seq + 1 - 2 * x, tp + 1 - 2 * c)
    into.start()

    def features(to):
        return remote(
            h_own, h_all.at[pl.ds(2 * tp, 2)], h_send.at[to], h_got.at[tp],
            2 * z + to // 2, 2 * (to % 2) + x,
        )

    own_features = pltpu.make_async_copy(h_own, h_all.at[pl.ds(2 * tp, 2)], h_got.at[tp])
    for to in range(4):
        itself = (x == c) & (x == to // 2) & (y == to % 2)

        @pl.when(itself)
        def _():
            own_features.start()

        @pl.when(jnp.logical_not(itself))
        def _():
            features(to).start()

    @pl.when(x == c)
    def _():
        par_local.start()

    @pl.when(x != c)
    def _():
        par_swap.start()

    into.turn(0)
    out_of.start()
    for far in range(1, planes):
        into.turn(far)
    out_of.turn(0)

    for quarter in range(4):
        remote(
            h_own, h_all.at[pl.ds(2 * quarter, 2)], h_send.at[0], h_got.at[quarter],
            seq, tp + 1 - 2 * c,
        ).wait_recv()

    @pl.when(x == c)
    def _():
        par_local.wait()

    @pl.when(x != c)
    def _():
        par_swap.wait()

    into.arrive()

    def project(start, size):
        total = jnp.zeros((tokens, size), f32)
        for block in range(2 * planes):
            total = total + jnp.dot(
                h_all[order_ref[block]], w_all[block, :, start : start + size],
                preferred_element_type=f32,
            )
        return total.astype(bf16)

    for part in range(0, mix_width, 512):
        done = project(part, 512)
        rows_ext[8:, part : part + 512] = done.astype(f32)
        edge_own[:, part : part + 512] = done[tokens - 16 :]

    def edge(to):
        return remote(edge_own, edge_got, edge_sems.at[0], edge_sems.at[1], *to)

    @pl.when(jnp.logical_not(last))
    def _():
        edge(after).start()

    gates[...] = project(mix_width, width)
    raw = project(step_at, w_own.shape[1] - step_at).astype(f32)

    lane_heads = lax.broadcasted_iota(jnp.int32, (1, 128), 1) < heads
    bias = jnp.where(lane_heads, par[5:6, 0:128], 0.0)
    rate = jnp.where(lane_heads, jnp.exp(par[6:7, 0:128]), 0.0)
    shifted = raw + bias
    dt = jnp.maximum(shifted, 0.0) + jnp.log1p(jnp.exp(-jnp.abs(shifted)))
    row_at = lax.broadcasted_iota(jnp.int32, (tokens, tokens), 0)
    column_at = lax.broadcasted_iota(jnp.int32, (tokens, tokens), 1)
    first_pos = (2 * z + c) * tokens
    ends = [lengths_ref[0]]
    for i in range(1, lengths_ref.shape[0]):
        ends.append(ends[-1] + lengths_ref[i])

    def segment(position):
        count = jnp.zeros_like(position)
        for end in ends:
            count = count + (position >= end).astype(jnp.int32)
        return count

    row_segments, column_segments = segment(first_pos + row_at), segment(first_pos + column_at)
    causal = (row_at >= column_at) & (row_segments == column_segments)
    lower = (row_at >= column_at).astype(f32)
    summed = jnp.dot(lower, -dt * rate, precision=HIGHEST_PREC, preferred_element_type=f32)
    summed_rows, dt_rows = jnp.transpose(summed), jnp.transpose(dt)
    positions = first_pos + lax.broadcasted_iota(jnp.int32, (tokens, 128), 0)
    segments = segment(positions)
    prev_segment = segment(jnp.full((tokens, 128), first_pos - 1, jnp.int32))
    last_segment = segment(jnp.full((tokens, 128), first_pos + tokens - 1, jnp.int32))
    carry_in = jnp.where(segments == prev_segment, jnp.exp(summed), 0.0)
    end_sum = summed[tokens - 1 : tokens]
    tail = jnp.where(segments == last_segment, jnp.exp(end_sum - summed), 0.0) * dt
    keep = jnp.where(last_segment[0:8] == prev_segment[0:8], jnp.exp(end_sum), 0.0)
    spread = (
        lax.broadcasted_iota(jnp.int32, (128, width), 1) // head_dim
        == lax.broadcasted_iota(jnp.int32, (128, width), 0)
    ).astype(f32)

    def over_channels(per_head):
        return jnp.dot(per_head, spread, precision=HIGHEST_PREC, preferred_element_type=f32)

    keep_rows = lax.dot_general(
        spread, keep, (((0,), (1,)), ((), ())), precision=HIGHEST_PREC, preferred_element_type=f32
    )[:, 0:1]

    @pl.when(first)
    def _():
        rows_ext[0:8] = jnp.zeros((8, mix_width), f32)

    @pl.when(jnp.logical_not(first))
    def _():
        edge(before).wait_recv()
        rows_ext[0:8] = edge_got[...].astype(f32)[8:16]

    def convolve(start, size, taps):
        total = jnp.zeros((tokens, size), f32)
        for k in range(4):
            back = 3 - k
            counted = (segment(positions - back) == segments) & (positions >= back)
            term = taps[k : k + 1] * rows_ext[8 - back : 8 - back + tokens, start : start + size]
            total = total + jnp.where(counted[:, 0:1], term, 0.0)
        return jax.nn.silu(total).astype(bf16)

    mixed[:, 0:width] = convolve(0, width, par[0:4])
    mixed[:, width:] = convolve(width, shared_width, shared_taps_ref[...])
    values = mixed[:, 0:width]
    b_rows = mixed[:, width : width + state_size]
    c_rows = mixed[:, width + state_size :]
    weighted = (values.astype(f32) * over_channels(tail)).astype(bf16)
    fresh[...] = lax.dot_general(
        weighted, b_rows, (((0,), (0,)), ((), ())), preferred_element_type=f32
    )

    def state(to):
        return remote(state_own, state_got, state_sems.at[0], state_sems.at[1], *to)

    @pl.when(first)
    def _():
        state_got[...] = jnp.zeros_like(state_got)
        state_own[...] = fresh[...].astype(bf16)
        state(after).start()

    out_of.turn(1)
    scores = lax.dot_general(c_rows, b_rows, (((1,), (1,)), ((), ())), preferred_element_type=f32)
    scores = jnp.where(causal, scores, 0.0)
    for head in range(heads):
        gap = summed[:, head : head + 1] - summed_rows[head : head + 1]
        weights = scores * jnp.exp(jnp.where(causal, gap, 0.0)) * dt_rows[head : head + 1]
        at = slice(head * head_dim, (head + 1) * head_dim)
        rows_ext[8:, at] = jnp.dot(
            weights.astype(bf16), mixed[:, at], preferred_element_type=f32
        )

    @pl.when(jnp.logical_not(first))
    def _():
        state(before).wait_recv()

        @pl.when(jnp.logical_not(last))
        def _():
            state_own[...] = (keep_rows * state_got[...].astype(f32) + fresh[...]).astype(bf16)
            state(after).start()

    for far in range(2, planes):
        out_of.turn(far)
    inter = lax.dot_general(
        c_rows, state_got[...], (((1,), (1,)), ((), ())), preferred_element_type=f32
    ) * over_channels(carry_in)
    skip = over_channels(
        jnp.broadcast_to(jnp.where(lane_heads, par[7:8, 0:128], 0.0), (8, 128))
    )[0:1]
    gated = (rows_ext[8:, 0:width] + inter + skip * values.astype(f32)) * jax.nn.silu(
        gates[...].astype(f32)
    )
    sums = lax.dot_general(
        jnp.ones((8, width), f32), gated * gated, (((1,), (1,)), ((), ())),
        precision=HIGHEST_PREC, preferred_element_type=f32,
    )
    sq_leaving[...] = sums
    scaled = (gated * par[4:5]).astype(bf16)
    out_of.arrive()
    columns = 2 * w_out_ref.shape[0]

    def outward(to):
        return remote(leaving.at[to], arrived.at[share], send.at[to], recv.at[share], 2 * z + c, to)

    def squares(to):
        return remote(
            sq_leaving, sq_arrived.at[share], sq_send.at[to], sq_recv.at[share], 2 * z + c, to
        )

    for to in range(4):
        product = lax.dot_general(
            scaled, o_all[2 * to : 2 * to + 2].reshape(columns, width),
            (((1,), (1,)), ((), ())), preferred_element_type=f32,
        ).astype(bf16)
        itself = (x == c) & (tp == to)

        @pl.when(itself)
        def _():
            arrived[share] = product
            sq_arrived[share] = sums

        @pl.when(jnp.logical_not(itself))
        def _():
            leaving[to] = product
            outward(to).start()
            squares(to).start()

    into.leave()
    out_of.leave()
    for to in range(4):
        itself = (x == c) & (x == to // 2) & (y == to % 2)

        @pl.when(jnp.logical_not(itself))
        def _():
            features(to).wait_send()

    @pl.when(jnp.logical_not(last))
    def _():
        edge(after).wait_send()
        state(after).wait_send()

    total, sq_total = 0.0, 0.0
    for slot in range(4):
        @pl.when(jnp.logical_not((x == c) & (share == slot)))
        def _():
            remote(
                leaving.at[0], arrived.at[slot], send.at[0], recv.at[slot], seq, tp + 1 - 2 * c
            ).wait_recv()
            remote(
                sq_leaving, sq_arrived.at[slot], sq_send.at[0], sq_recv.at[slot],
                seq, tp + 1 - 2 * c,
            ).wait_recv()

        total = total + arrived[slot].astype(f32)
        sq_total = sq_total + sq_arrived[slot]
    scale = lax.rsqrt(sq_total[0:1] / inner_total + EPSILON)
    scale_rows = jnp.transpose(jnp.broadcast_to(scale, (128, tokens)))[:, 0:1]
    out_ref[...] = (total * scale_rows).astype(out_ref.dtype)

    for to in range(4):
        itself = (x == c) & (tp == to)

        @pl.when(jnp.logical_not(itself))
        def _():
            outward(to).wait_send()
            squares(to).wait_send()


def on_device_paired(
    hidden_in,
    w_in_gate,
    w_in_value,
    w_in_shared,
    w_in_step,
    conv_value,
    conv_shared,
    dt_bias,
    a_log,
    skip_gain,
    norm_gain,
    w_out,
    prompt_lengths,
    row_blocks,
):
    blocks = lax.axis_size("seq")
    planes = blocks // 2
    tokens, features = hidden_in.shape
    rows, width = w_in_value.shape
    shared_width, heads = w_in_shared.shape[1], dt_bias.shape[0]
    mix_width = width + shared_width
    in_width = mix_width + width + 128
    state_size = shared_width // 2
    out_columns = w_out.shape[1]
    f32, bf16, dma = jnp.float32, jnp.bfloat16, pltpu.SemaphoreType.DMA
    vmem, smem = pl.BlockSpec(memory_space=pltpu.VMEM), pl.BlockSpec(memory_space=pltpu.SMEM)

    def relay_sems(chunks):
        return [dma((blocks, chunks)), dma((chunks,))] + [dma((planes, chunks))] * 3

    return pl.pallas_call(
        functools.partial(mixer_kernel, planes, heads, width * lax.axis_size("tp")),
        out_shape=jax.ShapeDtypeStruct((tokens, features), bf16),
        in_specs=[smem] * 2 + [vmem] * 12,
        out_specs=vmem,
        scratch_shapes=[
            pltpu.VMEM((rows, in_width), bf16),
            pltpu.VMEM((blocks, rows, in_width), bf16),
            pltpu.VMEM((blocks, out_columns, width), bf16),
            pltpu.VMEM((2, tokens, features // 2), bf16),
            pltpu.VMEM((8, tokens, features // 2), bf16),
            pltpu.VMEM((8, width), f32),
            pltpu.VMEM((8, width), f32),
            pltpu.VMEM((tokens, width), bf16),
            pltpu.VMEM((tokens + 8, mix_width), f32),
            pltpu.VMEM((16, mix_width), bf16),
            pltpu.VMEM((16, mix_width), bf16),
            pltpu.VMEM((tokens, mix_width), bf16),
            pltpu.VMEM((width, state_size), f32),
            pltpu.VMEM((width, state_size), bf16),
            pltpu.VMEM((width, state_size), bf16),
            pltpu.VMEM((4, tokens, features), bf16),
            pltpu.VMEM((4, tokens, features), bf16),
            pltpu.VMEM((8, tokens), f32),
            pltpu.VMEM((4, 8, tokens), f32),
        ]
        + relay_sems(rows // 48)
        + relay_sems(out_columns // 96)
        + [dma((4,)), dma((4,)), dma((2,)), dma((2,)), dma((2,))]
        + [dma((4,))] * 4,
        compiler_params=pltpu.CompilerParams(
            collective_id=0, has_side_effects=True, vmem_limit_bytes=50 << 20
        ),
        name="mixer",
    )(
        prompt_lengths,
        row_blocks,
        hidden_in,
        w_in_gate,
        w_in_value,
        w_in_shared,
        w_in_step,
        conv_value,
        conv_shared,
        dt_bias[None],
        a_log[None],
        skip_gain[None],
        norm_gain[None],
        w_out.astype(bf16).T,
    )


def paired(mesh):
    return dict(mesh.shape) == {"seq": 8, "tp": 4}


def solution(mesh):
    return jax.shard_map(
        on_device_paired if paired(mesh) else on_device_plain,
        mesh=mesh,
        in_specs=(
            P("seq", "tp"),
            P("seq", "tp"),
            P("seq", "tp"),
            P("seq", None),
            P("seq", "tp"),
            P(None, "tp"),
            P(),
            P("tp"),
            P("tp"),
            P("tp"),
            P("tp"),
            P("tp", "seq"),
            P(),
            P(),
        ),
        out_specs=P("seq", "tp"),
        check_vma=False,
    )
```

```python
import functools

import jax
import jax.numpy as jnp
from jax import lax
from jax.experimental import pallas as pl
from jax.experimental.pallas import tpu as pltpu
from jax.sharding import PartitionSpec as P

MESH = pl.DeviceIdType.MESH

EPSILON = 1e-05
HIGHEST_PREC = lax.Precision.HIGHEST


def passed_along(block, axis, distance):
    devices = range(lax.axis_size(axis))
    route = [(i - distance, i) for i in devices if i - distance in devices]
    return lax.ppermute(block, axis, route)


def prefix_2(x, axis, combine, identity):
    count, here = (lax.axis_size(axis), lax.axis_index(axis))
    everything = jax.tree.map(
        lambda part, kind: lax.all_gather(part.astype(kind), axis), x, (jnp.bfloat16, jnp.bfloat16)
    )
    start = jax.tree.map(
        lambda part, zero: jnp.broadcast_to(jnp.asarray(zero, part.dtype), part.shape), x, identity
    )

    def turn(k, before):
        reached = k < here
        new = combine(
            before, jax.tree.map(lambda part, own: part[k].astype(own.dtype), everything, x)
        )
        return jax.tree.map(lambda a, b: jnp.where(reached, a, b), new, before)

    return lax.fori_loop(0, count, turn, start)


def segment_of(positions, doc_ends):
    return jnp.sum((positions[:, None] >= doc_ends[None, :]).astype(jnp.int32), axis=1)


def span_parts(values, b_half, c_half, steps_dt, decay_rates, segments, prev_seg):
    length = values.shape[0]
    b_rows = b_half.astype(jnp.float32)
    cumulative = jnp.cumsum(-steps_dt * decay_rates[None, :], axis=0)
    places = jnp.arange(length)
    causal = (places[:, None] >= places[None, :]) & (segments[:, None] == segments[None, :])
    gaps_log = jnp.where(causal[:, :, None], cumulative[:, None, :] - cumulative[None, :, :], 0.0)
    decays_in = jnp.where(causal[:, :, None], jnp.exp(gaps_log), 0.0)
    scores = jnp.dot(c_half, b_half.T, preferred_element_type=jnp.float32)
    weights = scores[:, :, None] * decays_in * steps_dt[None, :, :]
    intra_part = jnp.einsum("ijh,jhp->ihp", weights, values, precision=HIGHEST_PREC)
    carry_in = jnp.where((segments == prev_seg)[:, None], jnp.exp(cumulative), 0.0)
    tail_weight = (
        jnp.where(
            (segments == segments[-1])[:, None], jnp.exp(cumulative[-1][None, :] - cumulative), 0.0
        )
        * steps_dt
    )
    fresh_state = jnp.einsum("jh,jhp,jn->hpn", tail_weight, values, b_rows, precision=HIGHEST_PREC)
    keep_factor = jnp.where(segments[-1] == prev_seg, jnp.exp(cumulative[-1]), 0.0)
    return (intra_part, carry_in, fresh_state, keep_factor)


def combine(earlier, later):
    return (earlier[0] * later[0], later[0][:, None, None] * earlier[1] + later[1])


def on_device_plain(
    hidden_in,
    w_in_gate,
    w_in_value,
    w_in_shared,
    w_in_step,
    conv_value,
    conv_shared,
    dt_bias,
    a_log,
    skip_gain,
    norm_gain,
    w_out,
    prompt_lengths,
    row_blocks,
):
    seq_count = lax.axis_size("seq")
    tokens_here = hidden_in.shape[0]
    edge_count = conv_value.shape[0] - 1
    gathered = lax.all_gather(hidden_in, "tp", axis=1, tiled=True)
    row_count = gathered.shape[0]
    model_width = gathered.shape[1]
    permuted = jnp.take(
        gathered.reshape(row_count, seq_count, model_width // seq_count), row_blocks, axis=1
    ).reshape(row_count, model_width)
    stored = (
        w_in_gate.astype(jnp.bfloat16),
        w_in_value.astype(jnp.bfloat16),
        w_in_shared.astype(jnp.bfloat16),
        w_in_step.astype(jnp.bfloat16),
    )
    pieces = (
        lax.all_gather(stored[0], "seq", axis=0, tiled=True),
        lax.all_gather(stored[1], "seq", axis=0, tiled=True),
        lax.all_gather(stored[2], "seq", axis=0, tiled=True),
        lax.all_gather(stored[3], "seq", axis=0, tiled=True),
    )
    projected = tuple(
        (
            jnp.dot(permuted, weight_piece, preferred_element_type=jnp.float32)
            for weight_piece in pieces
        )
    )
    gate_all, value_all, shared_all, raw_all = [result.astype(jnp.bfloat16) for result in projected]
    mixed_in = jnp.concatenate([value_all, shared_all], axis=1)
    edge_mix = passed_along(mixed_in[tokens_here - edge_count :], "seq", 1)
    doc_ends = jnp.cumsum(prompt_lengths)
    first_pos = lax.axis_index("seq") * tokens_here
    positions = first_pos + jnp.arange(tokens_here, dtype=jnp.int32)
    edge_positions = first_pos - edge_count + jnp.arange(edge_count, dtype=jnp.int32)
    segments = segment_of(positions, doc_ends)
    ext_segments = jnp.concatenate([segment_of(edge_positions, doc_ends), segments])
    ext_rows = jnp.concatenate([edge_mix, mixed_in], axis=0)
    kernel = jnp.concatenate([conv_value, conv_shared], axis=1)
    conv_sum = jnp.zeros(mixed_in.shape, jnp.float32)
    for tap_index in range(edge_count + 1):
        same_doc = (ext_segments[tap_index : tap_index + tokens_here] == segments)[:, None]
        conv_sum = conv_sum + jnp.where(
            same_doc,
            kernel[tap_index][None, :]
            * ext_rows[tap_index : tap_index + tokens_here].astype(jnp.float32),
            0.0,
        )
    convolved = jax.nn.silu(conv_sum).astype(jnp.bfloat16)
    local_inner = conv_value.shape[1]
    local_heads = dt_bias.shape[0]
    head_dim = local_inner // local_heads
    state_size = conv_shared.shape[1] // 2
    values = (
        convolved[:, :local_inner].astype(jnp.float32).reshape(tokens_here, local_heads, head_dim)
    )
    b_half = convolved[:, local_inner : local_inner + state_size]
    c_half = convolved[:, local_inner + state_size :]
    c_rows = c_half.astype(jnp.float32)
    steps_dt = jax.nn.softplus(raw_all.astype(jnp.float32) + dt_bias[None, :])
    decay_rates = jnp.exp(a_log)
    prev_first = segment_of(jnp.reshape(first_pos - 1, (1,)), doc_ends)[0]
    device_keep = jnp.ones((local_heads,), jnp.float32)
    device_state = jnp.zeros((local_heads, head_dim, state_size), jnp.float32)
    parts = span_parts(values, b_half, c_half, steps_dt, decay_rates, segments, prev_first)
    device_keep = parts[3] * device_keep
    device_state = parts[3][:, None, None] * device_state + parts[2]
    identity = (jnp.ones_like(device_keep), jnp.zeros_like(device_state))
    prefix = prefix_2((device_keep, device_state), "seq", combine, identity)
    carried = prefix[1]
    intra_part, carry_in, fresh_state, keep_factor = parts
    inter_part = (
        jnp.einsum("in,hpn->ihp", c_rows, carried, precision=HIGHEST_PREC) * carry_in[:, :, None]
    )
    outputs = intra_part + inter_part
    mixed_heads = outputs + skip_gain[None, :, None] * values
    gated = mixed_heads.reshape(tokens_here, local_inner) * jax.nn.silu(
        gate_all.astype(jnp.float32)
    )
    squares = jnp.sum(gated * gated, axis=1)
    square_total = lax.psum(squares, "tp")
    mean_square = square_total / (local_inner * lax.axis_size("tp"))
    normed = (gated * lax.rsqrt(mean_square + EPSILON)[:, None] * norm_gain[None, :]).astype(
        jnp.bfloat16
    )
    out_weight = w_out.astype(jnp.bfloat16)
    partial_terms = jnp.dot(
        normed,
        lax.all_gather(out_weight, "seq", axis=1, tiled=True),
        preferred_element_type=jnp.float32,
    )
    return lax.psum_scatter(
        partial_terms.astype(jnp.bfloat16), "tp", scatter_dimension=1, tiled=True
    )


def place():
    seq, tp = lax.axis_index("seq"), lax.axis_index("tp")
    return seq, tp, seq // 2, seq % 2, tp // 2, tp % 2


def remote(src, dst, send, recv, seq, tp):
    return pltpu.make_async_remote_copy(
        src_ref=src, dst_ref=dst, send_sem=send, recv_sem=recv,
        device_id=(seq, tp), device_id_type=MESH,
    )


def greet(planes):
    seq, tp, z, x, y, c = place()
    barrier = pltpu.get_barrier_semaphore()

    def meet(to_seq, to_tp):
        pl.semaphore_signal(barrier, inc=1, device_id=(to_seq, to_tp), device_id_type=MESH)

    for other in range(1, 8):
        dx, dt = other // 4, other % 4
        meet(2 * z + (x + dx) % 2, (tp + dt) % 4)

    @pl.when(z > 0)
    def _():
        meet(seq - 2, tp)

        @pl.when(c == 0)
        def _():
            meet(seq - 2, tp + 1)

    @pl.when(z < planes - 1)
    def _():
        meet(seq + 2, tp)

        @pl.when(c == 1)
        def _():
            meet(seq + 2, tp - 1)

    below = jnp.where(z > 0, 2 - c, 0)
    above = jnp.where(z < planes - 1, 1 + c, 0)
    pl.semaphore_wait(barrier, 7 + below + above)


class Relay:
    def __init__(self, planes, depth, own, every, sems):
        self.planes, self.depth, self.own, self.every = planes, depth, own, every
        self.got, self.swapped, self.up, self.down, self.across = sems
        self.chunks = own.shape[0] // depth
        self.at = place()

    def rows(self, k):
        return pl.ds(pl.multiple_of(k * self.depth, self.depth), self.depth)

    def local(self, k):
        seq, tp, z, x, y, c = self.at
        return pltpu.make_async_copy(
            self.own.at[self.rows(k)], self.every.at[2 * z + c, self.rows(k)], self.got.at[2 * z + c, k]
        )

    def swap(self, k):
        seq, tp, z, x, y, c = self.at
        slot = 2 * z + 1 - c
        return remote(
            self.own.at[self.rows(k)], self.every.at[slot, self.rows(k)],
            self.swapped.at[k], self.got.at[slot, k], seq + 1 - 2 * x, tp + 1 - 2 * c,
        )

    def sent(self, slot, k, sems, to_seq, to_tp):
        here = self.every.at[slot, self.rows(k)]
        return remote(here, here, sems.at[slot // 2, k], self.got.at[slot, k], to_seq, to_tp)

    def going_up(self, slot, k):
        return self.sent(slot, k, self.up, self.at[0] + 2, self.at[1])

    def going_down(self, slot, k):
        return self.sent(slot, k, self.down, self.at[0] - 2, self.at[1])

    def going_across(self, slot, k):
        return self.sent(slot, k, self.across, self.at[0], self.at[1] + 1 - 2 * self.at[5])

    def start(self):
        seq, tp, z, x, y, c = self.at

        @pl.when(x == c)
        def _():
            @pl.loop(0, self.chunks)
            def _(k):
                self.local(k).start()

        @pl.when(x != c)
        def _():
            @pl.loop(0, self.chunks)
            def _(k):
                self.swap(k).start()

    def turn(self, far):
        seq, tp, z, x, y, c = self.at
        mine = 2 * z + c

        @pl.loop(0, self.chunks)
        def _(k):
            if far == 0:
                @pl.when(x == c)
                def _():
                    self.local(k).wait()

                @pl.when(x != c)
                def _():
                    self.going_across(mine, k).wait_recv()

                @pl.when(z < self.planes - 1)
                def _():
                    self.going_up(mine, k).start()

                @pl.when(z > 0)
                def _():
                    self.going_down(mine, k).start()

                self.going_across(mine, k).start()
            else:
                @pl.when(z >= far)
                def _():
                    slot = mine - 2 * far
                    self.going_across(slot, k).wait_recv()

                    @pl.when(z < self.planes - 1)
                    def _():
                        self.going_up(slot, k).start()

                    self.going_across(slot, k).start()

                @pl.when(z < self.planes - far)
                def _():
                    slot = mine + 2 * far
                    self.going_across(slot, k).wait_recv()

                    @pl.when(z > 0)
                    def _():
                        self.going_down(slot, k).start()

                    self.going_across(slot, k).start()

    def arrive(self, planes):
        c = self.at[5]

        @pl.loop(0, self.chunks)
        def _(k):
            for at in planes:
                self.going_across(2 * at + 1 - c, k).wait_recv()

    def leave(self):
        seq, tp, z, x, y, c = self.at

        @pl.loop(0, self.chunks)
        def _(k):
            for at in range(self.planes):
                slot = 2 * at + c
                self.going_across(slot, k).wait_send()

                @pl.when((z < self.planes - 1) & (z >= at))
                def _():
                    self.going_up(slot, k).wait_send()

                @pl.when((z > 0) & (z <= at))
                def _():
                    self.going_down(slot, k).wait_send()

            @pl.when(x != c)
            def _():
                self.swap(k).wait_send()


def mixer_kernel(
    planes, heads, inner_total,
    lengths_ref, order_ref, h_ref, gate_ref, value_ref, shared_ref, step_ref, taps_ref,
    shared_taps_ref, bias_ref, log_ref, skip_ref, gain_ref, w_out_ref, out_ref,
    w_own, w_all, o_own, o_all, acc, h_own, h_all, p_own, par, gates, rows_ext, edge_own, edge_got, mixed,
    fresh, state_got, state_own, leaving, arrived, sq_leaving, sq_arrived,
    w_got, w_swapped, w_up, w_down, w_across, o_got, o_swapped, o_up, o_down, o_across,
    h_send, h_got, p_sems, edge_sems, state_sems, send, recv, sq_send, sq_recv,
):
    f32, bf16 = jnp.float32, jnp.bfloat16
    seq, tp, z, x, y, c = place()
    share = 2 * y + x
    first, last = (z == 0) & (c == 0), (z == planes - 1) & (c == 1)
    before = (seq - 2 * (1 - c), tp + 1 - 2 * c)
    after = (seq + 2 * c, tp + 1 - 2 * c)
    tokens, width = h_ref.shape[0], value_ref.shape[1]
    shared_width = shared_ref.shape[1]
    mix_width, state_size, head_dim = width + shared_width, shared_width // 2, width // heads
    half_features = h_ref.shape[1] // 2
    step_at = mix_width + width

    w_own[:, 0:width] = value_ref[...].astype(bf16)
    w_own[:, width:mix_width] = shared_ref[...].astype(bf16)
    w_own[:, mix_width:step_at] = gate_ref[...].astype(bf16)
    w_own[:, step_at:] = jnp.zeros((w_own.shape[0], w_own.shape[1] - step_at), bf16)
    w_own[:, step_at : step_at + heads] = step_ref[...].astype(bf16)
    h_own[0] = h_ref[:, 0:half_features]
    h_own[1] = h_ref[:, half_features:]
    p_own[...] = jnp.zeros_like(p_own)
    p_own[0:4, :] = taps_ref[...]
    p_own[4:5, :] = gain_ref[...]
    p_own[5:6, 0:heads] = bias_ref[...]
    p_own[6:7, 0:heads] = log_ref[...]
    p_own[7:8, 0:heads] = skip_ref[...]
    greet(planes)

    into = Relay(planes, 48, w_own, w_all, (w_got, w_swapped, w_up, w_down, w_across))
    out_of = Relay(planes, 96, o_own, o_all, (o_got, o_swapped, o_up, o_down, o_across))
    par_local = pltpu.make_async_copy(p_own, par, p_sems.at[0])
    par_swap = remote(p_own, par, p_sems.at[1], p_sems.at[0], seq + 1 - 2 * x, tp + 1 - 2 * c)
    into.start()

    def features(to):
        return remote(
            h_own, h_all.at[pl.ds(2 * tp, 2)], h_send.at[to], h_got.at[tp],
            2 * z + to // 2, 2 * (to % 2) + x,
        )

    own_features = pltpu.make_async_copy(h_own, h_all.at[pl.ds(2 * tp, 2)], h_got.at[tp])
    for to in range(4):
        itself = (x == c) & (x == to // 2) & (y == to % 2)

        @pl.when(itself)
        def _():
            own_features.start()

        @pl.when(jnp.logical_not(itself))
        def _():
            features(to).start()

    @pl.when(x == c)
    def _():
        par_local.start()

    @pl.when(x != c)
    def _():
        par_swap.start()

    into.turn(0)
    square = (w_out_ref.shape[0], w_out_ref.shape[0])
    unit = lax.broadcasted_iota(jnp.int32, square, 0) == lax.broadcasted_iota(jnp.int32, square, 1)
    o_own[...] = lax.dot_general(
        w_out_ref[...].astype(bf16), unit.astype(f32).astype(bf16), (((0,), (0,)), ((), ())),
        preferred_element_type=f32,
    ).astype(bf16)
    out_of.start()
    inside = (z > 0) & (z < planes - 1)
    outside = jnp.logical_not(inside)

    @pl.when(outside)
    def _():
        out_of.turn(0)

    for far in range(1, planes - 1):
        into.turn(far)

    @pl.when(inside)
    def _():
        out_of.turn(0)
        out_of.turn(1)

    for quarter in range(4):
        remote(
            h_own, h_all.at[pl.ds(2 * quarter, 2)], h_send.at[0], h_got.at[quarter],
            seq, tp + 1 - 2 * c,
        ).wait_recv()

    @pl.when(x == c)
    def _():
        par_local.wait()

    @pl.when(x != c)
    def _():
        par_swap.wait()

    nearest = [jnp.where(z < planes // 2, i, planes - 1 - i) for i in range(planes)]

    def project(start, size, part):
        total = jnp.zeros((tokens, size), f32)
        for plane in part:
            for block in (2 * plane, 2 * plane + 1):
                total = total + jnp.dot(
                    h_all[order_ref[block]], w_all[block, :, start : start + size],
                    preferred_element_type=f32,
                )
        return total

    into.arrive(nearest[:-1])
    for part in range(0, acc.shape[1], 384):
        acc[:, part : part + 384] = project(part, 384, nearest[:-1])
    into.turn(planes - 1)
    into.arrive(nearest[-1:])

    def projected(start, size):
        return (acc[:, start : start + size] + project(start, size, nearest[-1:])).astype(bf16)

    for part in range(0, mix_width, 512):
        done = projected(part, 512)
        rows_ext[8:, part : part + 512] = done.astype(f32)
        edge_own[:, part : part + 512] = done[tokens - 16 :]

    def edge(to):
        return remote(edge_own, edge_got, edge_sems.at[0], edge_sems.at[1], *to)

    @pl.when(jnp.logical_not(last))
    def _():
        edge(after).start()

    gates[...] = projected(mix_width, width)
    raw = projected(step_at, w_own.shape[1] - step_at).astype(f32)

    lane_heads = lax.broadcasted_iota(jnp.int32, (1, 128), 1) < heads
    bias = jnp.where(lane_heads, par[5:6, 0:128], 0.0)
    rate = jnp.where(lane_heads, jnp.exp(par[6:7, 0:128]), 0.0)
    shifted = raw + bias
    dt = jnp.maximum(shifted, 0.0) + jnp.log1p(jnp.exp(-jnp.abs(shifted)))
    row_at = lax.broadcasted_iota(jnp.int32, (tokens, tokens), 0)
    column_at = lax.broadcasted_iota(jnp.int32, (tokens, tokens), 1)
    first_pos = (2 * z + c) * tokens
    ends = [lengths_ref[0]]
    for i in range(1, lengths_ref.shape[0]):
        ends.append(ends[-1] + lengths_ref[i])

    def segment(position):
        count = jnp.zeros_like(position)
        for end in ends:
            count = count + (position >= end).astype(jnp.int32)
        return count

    row_segments, column_segments = segment(first_pos + row_at), segment(first_pos + column_at)
    causal = (row_at >= column_at) & (row_segments == column_segments)
    lower = (row_at >= column_at).astype(f32)
    summed = jnp.dot(lower, -dt * rate, precision=HIGHEST_PREC, preferred_element_type=f32)
    summed_rows, dt_rows = jnp.transpose(summed), jnp.transpose(dt)
    positions = first_pos + lax.broadcasted_iota(jnp.int32, (tokens, 128), 0)
    segments = segment(positions)
    prev_segment = segment(jnp.full((tokens, 128), first_pos - 1, jnp.int32))
    last_segment = segment(jnp.full((tokens, 128), first_pos + tokens - 1, jnp.int32))
    carry_in = jnp.where(segments == prev_segment, jnp.exp(summed), 0.0)
    end_sum = summed[tokens - 1 : tokens]
    tail = jnp.where(segments == last_segment, jnp.exp(end_sum - summed), 0.0) * dt
    keep = jnp.where(last_segment[0:8] == prev_segment[0:8], jnp.exp(end_sum), 0.0)
    spread = (
        lax.broadcasted_iota(jnp.int32, (128, width), 1) // head_dim
        == lax.broadcasted_iota(jnp.int32, (128, width), 0)
    ).astype(f32)

    def over_channels(per_head):
        return jnp.dot(per_head, spread, precision=HIGHEST_PREC, preferred_element_type=f32)

    keep_rows = lax.dot_general(
        spread, keep, (((0,), (1,)), ((), ())), precision=HIGHEST_PREC, preferred_element_type=f32
    )[:, 0:1]

    @pl.when(first)
    def _():
        rows_ext[0:8] = jnp.zeros((8, mix_width), f32)

    @pl.when(jnp.logical_not(first))
    def _():
        edge(before).wait_recv()
        rows_ext[0:8] = edge_got[...].astype(f32)[8:16]

    def convolve(start, size, taps):
        total = jnp.zeros((tokens, size), f32)
        for k in range(4):
            back = 3 - k
            counted = (segment(positions - back) == segments) & (positions >= back)
            term = taps[k : k + 1] * rows_ext[8 - back : 8 - back + tokens, start : start + size]
            total = total + jnp.where(counted[:, 0:1], term, 0.0)
        return jax.nn.silu(total).astype(bf16)

    mixed[:, 0:width] = convolve(0, width, par[0:4])
    mixed[:, width:] = convolve(width, shared_width, shared_taps_ref[...])
    values = mixed[:, 0:width]
    b_rows = mixed[:, width : width + state_size]
    c_rows = mixed[:, width + state_size :]
    weighted = (values.astype(f32) * over_channels(tail)).astype(bf16)
    fresh[...] = lax.dot_general(
        weighted, b_rows, (((0,), (0,)), ((), ())), preferred_element_type=f32
    )

    parts = 4
    depth = width // parts

    def state(part, to):
        at = pl.ds(part * depth, depth)
        return remote(
            state_own.at[at], state_got.at[at], state_sems.at[0, part], state_sems.at[1, part], *to
        )

    @pl.when(first)
    def _():
        state_got[...] = jnp.zeros_like(state_got)
        state_own[...] = fresh[...].astype(bf16)
        for part in range(parts):
            state(part, after).start()

    @pl.when(inside)
    def _():
        out_of.turn(2)

    @pl.when(outside)
    def _():
        out_of.turn(1)

    scores = lax.dot_general(c_rows, b_rows, (((1,), (1,)), ((), ())), preferred_element_type=f32)
    scores = jnp.where(causal, scores, 0.0)
    for head in range(heads):
        gap = summed[:, head : head + 1] - summed_rows[head : head + 1]
        weights = scores * jnp.exp(jnp.where(causal, gap, 0.0)) * dt_rows[head : head + 1]
        at = slice(head * head_dim, (head + 1) * head_dim)
        rows_ext[8:, at] = jnp.dot(
            weights.astype(bf16), mixed[:, at], preferred_element_type=f32
        )

    @pl.when(jnp.logical_not(first))
    def _():
        for part in range(parts):
            state(part, before).wait_recv()

            @pl.when(jnp.logical_not(last))
            def _():
                at = slice(part * depth, (part + 1) * depth)
                state_own[at] = (
                    keep_rows[at] * state_got[at].astype(f32) + fresh[at]
                ).astype(bf16)
                state(part, after).start()

    @pl.when(outside)
    def _():
        for far in range(2, planes):
            out_of.turn(far)

    inter = lax.dot_general(
        c_rows, state_got[...], (((1,), (1,)), ((), ())), preferred_element_type=f32
    ) * over_channels(carry_in)
    skip = over_channels(
        jnp.broadcast_to(jnp.where(lane_heads, par[7:8, 0:128], 0.0), (8, 128))
    )[0:1]
    gated = (rows_ext[8:, 0:width] + inter + skip * values.astype(f32)) * jax.nn.silu(
        gates[...].astype(f32)
    )
    sums = lax.dot_general(
        jnp.ones((8, width), f32), gated * gated, (((1,), (1,)), ((), ())),
        precision=HIGHEST_PREC, preferred_element_type=f32,
    )
    sq_leaving[...] = sums
    scaled = (gated * par[4:5]).astype(bf16)
    out_of.arrive(range(planes))
    columns = 2 * w_out_ref.shape[1]

    def outward(to):
        return remote(leaving.at[to], arrived.at[share], send.at[to], recv.at[share], 2 * z + c, to)

    def squares(to):
        return remote(
            sq_leaving, sq_arrived.at[share], sq_send.at[to], sq_recv.at[share], 2 * z + c, to
        )

    for to in range(4):
        product = lax.dot_general(
            scaled, o_all[2 * to : 2 * to + 2].reshape(columns, width),
            (((1,), (1,)), ((), ())), preferred_element_type=f32,
        ).astype(bf16)
        itself = (x == c) & (tp == to)

        @pl.when(itself)
        def _():
            arrived[share] = product
            sq_arrived[share] = sums

        @pl.when(jnp.logical_not(itself))
        def _():
            leaving[to] = product
            outward(to).start()
            squares(to).start()

    into.leave()
    out_of.leave()
    for to in range(4):
        itself = (x == c) & (x == to // 2) & (y == to % 2)

        @pl.when(jnp.logical_not(itself))
        def _():
            features(to).wait_send()

    @pl.when(jnp.logical_not(last))
    def _():
        edge(after).wait_send()
        for part in range(parts):
            state(part, after).wait_send()

    total, sq_total = 0.0, 0.0
    for slot in range(4):
        @pl.when(jnp.logical_not((x == c) & (share == slot)))
        def _():
            remote(
                leaving.at[0], arrived.at[slot], send.at[0], recv.at[slot], seq, tp + 1 - 2 * c
            ).wait_recv()
            remote(
                sq_leaving, sq_arrived.at[slot], sq_send.at[0], sq_recv.at[slot],
                seq, tp + 1 - 2 * c,
            ).wait_recv()

        total = total + arrived[slot].astype(f32)
        sq_total = sq_total + sq_arrived[slot]
    scale = lax.rsqrt(sq_total[0:1] / inner_total + EPSILON)
    scale_rows = jnp.transpose(jnp.broadcast_to(scale, (128, tokens)))[:, 0:1]
    out_ref[...] = (total * scale_rows).astype(out_ref.dtype)

    for to in range(4):
        itself = (x == c) & (tp == to)

        @pl.when(jnp.logical_not(itself))
        def _():
            outward(to).wait_send()
            squares(to).wait_send()


def on_device_paired(
    hidden_in,
    w_in_gate,
    w_in_value,
    w_in_shared,
    w_in_step,
    conv_value,
    conv_shared,
    dt_bias,
    a_log,
    skip_gain,
    norm_gain,
    w_out,
    prompt_lengths,
    row_blocks,
):
    blocks = lax.axis_size("seq")
    planes = blocks // 2
    tokens, features = hidden_in.shape
    rows, width = w_in_value.shape
    shared_width, heads = w_in_shared.shape[1], dt_bias.shape[0]
    mix_width = width + shared_width
    in_width = mix_width + width + 128
    state_size = shared_width // 2
    out_columns = w_out.shape[1]
    f32, bf16, dma = jnp.float32, jnp.bfloat16, pltpu.SemaphoreType.DMA
    vmem, smem = pl.BlockSpec(memory_space=pltpu.VMEM), pl.BlockSpec(memory_space=pltpu.SMEM)

    def relay_sems(chunks):
        return [dma((blocks, chunks)), dma((chunks,))] + [dma((planes, chunks))] * 3

    return pl.pallas_call(
        functools.partial(mixer_kernel, planes, heads, width * lax.axis_size("tp")),
        out_shape=jax.ShapeDtypeStruct((tokens, features), bf16),
        in_specs=[smem] * 2 + [vmem] * 12,
        out_specs=vmem,
        scratch_shapes=[
            pltpu.VMEM((rows, in_width), bf16),
            pltpu.VMEM((blocks, rows, in_width), bf16),
            pltpu.VMEM((out_columns, width), bf16),
            pltpu.VMEM((blocks, out_columns, width), bf16),
            pltpu.VMEM((tokens, in_width), f32),
            pltpu.VMEM((2, tokens, features // 2), bf16),
            pltpu.VMEM((8, tokens, features // 2), bf16),
            pltpu.VMEM((8, width), f32),
            pltpu.VMEM((8, width), f32),
            pltpu.VMEM((tokens, width), bf16),
            pltpu.VMEM((tokens + 8, mix_width), f32),
            pltpu.VMEM((16, mix_width), bf16),
            pltpu.VMEM((16, mix_width), bf16),
            pltpu.VMEM((tokens, mix_width), bf16),
            pltpu.VMEM((width, state_size), f32),
            pltpu.VMEM((width, state_size), bf16),
            pltpu.VMEM((width, state_size), bf16),
            pltpu.VMEM((4, tokens, features), bf16),
            pltpu.VMEM((4, tokens, features), bf16),
            pltpu.VMEM((8, tokens), f32),
            pltpu.VMEM((4, 8, tokens), f32),
        ]
        + relay_sems(rows // 48)
        + relay_sems(out_columns // 96)
        + [dma((4,)), dma((4,)), dma((2,)), dma((2,)), dma((2, 4))]
        + [dma((4,))] * 4,
        compiler_params=pltpu.CompilerParams(
            collective_id=0, has_side_effects=True, vmem_limit_bytes=50 << 20
        ),
        name="mixer",
    )(
        prompt_lengths,
        row_blocks,
        hidden_in,
        w_in_gate,
        w_in_value,
        w_in_shared,
        w_in_step,
        conv_value,
        conv_shared,
        dt_bias[None],
        a_log[None],
        skip_gain[None],
        norm_gain[None],
        w_out,
    )


def paired(mesh):
    return dict(mesh.shape) == {"seq": 8, "tp": 4}


def solution(mesh):
    return jax.shard_map(
        on_device_paired if paired(mesh) else on_device_plain,
        mesh=mesh,
        in_specs=(
            P("seq", "tp"),
            P("seq", "tp"),
            P("seq", "tp"),
            P("seq", None),
            P("seq", "tp"),
            P(None, "tp"),
            P(),
            P("tp"),
            P("tp"),
            P("tp"),
            P("tp"),
            P("tp", "seq"),
            P(),
            P(),
        ),
        out_specs=P("seq", "tp"),
        check_vma=False,
    )
```

```python
import functools

import jax
import jax.numpy as jnp
from jax import lax
from jax.experimental import pallas as pl
from jax.experimental.pallas import tpu as pltpu
from jax.sharding import PartitionSpec as P

MESH = pl.DeviceIdType.MESH

EPSILON = 1e-05
HIGHEST_PREC = lax.Precision.HIGHEST


def passed_along(block, axis, distance):
    devices = range(lax.axis_size(axis))
    route = [(i - distance, i) for i in devices if i - distance in devices]
    return lax.ppermute(block, axis, route)


def prefix_2(x, axis, combine, identity):
    count, here = (lax.axis_size(axis), lax.axis_index(axis))
    everything = jax.tree.map(
        lambda part, kind: lax.all_gather(part.astype(kind), axis), x, (jnp.bfloat16, jnp.bfloat16)
    )
    start = jax.tree.map(
        lambda part, zero: jnp.broadcast_to(jnp.asarray(zero, part.dtype), part.shape), x, identity
    )

    def turn(k, before):
        reached = k < here
        new = combine(
            before, jax.tree.map(lambda part, own: part[k].astype(own.dtype), everything, x)
        )
        return jax.tree.map(lambda a, b: jnp.where(reached, a, b), new, before)

    return lax.fori_loop(0, count, turn, start)


def segment_of(positions, doc_ends):
    return jnp.sum((positions[:, None] >= doc_ends[None, :]).astype(jnp.int32), axis=1)


def span_parts(values, b_half, c_half, steps_dt, decay_rates, segments, prev_seg):
    length = values.shape[0]
    b_rows = b_half.astype(jnp.float32)
    cumulative = jnp.cumsum(-steps_dt * decay_rates[None, :], axis=0)
    places = jnp.arange(length)
    causal = (places[:, None] >= places[None, :]) & (segments[:, None] == segments[None, :])
    gaps_log = jnp.where(causal[:, :, None], cumulative[:, None, :] - cumulative[None, :, :], 0.0)
    decays_in = jnp.where(causal[:, :, None], jnp.exp(gaps_log), 0.0)
    scores = jnp.dot(c_half, b_half.T, preferred_element_type=jnp.float32)
    weights = scores[:, :, None] * decays_in * steps_dt[None, :, :]
    intra_part = jnp.einsum("ijh,jhp->ihp", weights, values, precision=HIGHEST_PREC)
    carry_in = jnp.where((segments == prev_seg)[:, None], jnp.exp(cumulative), 0.0)
    tail_weight = (
        jnp.where(
            (segments == segments[-1])[:, None], jnp.exp(cumulative[-1][None, :] - cumulative), 0.0
        )
        * steps_dt
    )
    fresh_state = jnp.einsum("jh,jhp,jn->hpn", tail_weight, values, b_rows, precision=HIGHEST_PREC)
    keep_factor = jnp.where(segments[-1] == prev_seg, jnp.exp(cumulative[-1]), 0.0)
    return (intra_part, carry_in, fresh_state, keep_factor)


def combine(earlier, later):
    return (earlier[0] * later[0], later[0][:, None, None] * earlier[1] + later[1])


def on_device_plain(
    hidden_in,
    w_in_gate,
    w_in_value,
    w_in_shared,
    w_in_step,
    conv_value,
    conv_shared,
    dt_bias,
    a_log,
    skip_gain,
    norm_gain,
    w_out,
    prompt_lengths,
    row_blocks,
):
    seq_count = lax.axis_size("seq")
    tokens_here = hidden_in.shape[0]
    edge_count = conv_value.shape[0] - 1
    gathered = lax.all_gather(hidden_in, "tp", axis=1, tiled=True)
    row_count = gathered.shape[0]
    model_width = gathered.shape[1]
    permuted = jnp.take(
        gathered.reshape(row_count, seq_count, model_width // seq_count), row_blocks, axis=1
    ).reshape(row_count, model_width)
    stored = (
        w_in_gate.astype(jnp.bfloat16),
        w_in_value.astype(jnp.bfloat16),
        w_in_shared.astype(jnp.bfloat16),
        w_in_step.astype(jnp.bfloat16),
    )
    pieces = (
        lax.all_gather(stored[0], "seq", axis=0, tiled=True),
        lax.all_gather(stored[1], "seq", axis=0, tiled=True),
        lax.all_gather(stored[2], "seq", axis=0, tiled=True),
        lax.all_gather(stored[3], "seq", axis=0, tiled=True),
    )
    projected = tuple(
        (
            jnp.dot(permuted, weight_piece, preferred_element_type=jnp.float32)
            for weight_piece in pieces
        )
    )
    gate_all, value_all, shared_all, raw_all = [result.astype(jnp.bfloat16) for result in projected]
    mixed_in = jnp.concatenate([value_all, shared_all], axis=1)
    edge_mix = passed_along(mixed_in[tokens_here - edge_count :], "seq", 1)
    doc_ends = jnp.cumsum(prompt_lengths)
    first_pos = lax.axis_index("seq") * tokens_here
    positions = first_pos + jnp.arange(tokens_here, dtype=jnp.int32)
    edge_positions = first_pos - edge_count + jnp.arange(edge_count, dtype=jnp.int32)
    segments = segment_of(positions, doc_ends)
    ext_segments = jnp.concatenate([segment_of(edge_positions, doc_ends), segments])
    ext_rows = jnp.concatenate([edge_mix, mixed_in], axis=0)
    kernel = jnp.concatenate([conv_value, conv_shared], axis=1)
    conv_sum = jnp.zeros(mixed_in.shape, jnp.float32)
    for tap_index in range(edge_count + 1):
        same_doc = (ext_segments[tap_index : tap_index + tokens_here] == segments)[:, None]
        conv_sum = conv_sum + jnp.where(
            same_doc,
            kernel[tap_index][None, :]
            * ext_rows[tap_index : tap_index + tokens_here].astype(jnp.float32),
            0.0,
        )
    convolved = jax.nn.silu(conv_sum).astype(jnp.bfloat16)
    local_inner = conv_value.shape[1]
    local_heads = dt_bias.shape[0]
    head_dim = local_inner // local_heads
    state_size = conv_shared.shape[1] // 2
    values = (
        convolved[:, :local_inner].astype(jnp.float32).reshape(tokens_here, local_heads, head_dim)
    )
    b_half = convolved[:, local_inner : local_inner + state_size]
    c_half = convolved[:, local_inner + state_size :]
    c_rows = c_half.astype(jnp.float32)
    steps_dt = jax.nn.softplus(raw_all.astype(jnp.float32) + dt_bias[None, :])
    decay_rates = jnp.exp(a_log)
    prev_first = segment_of(jnp.reshape(first_pos - 1, (1,)), doc_ends)[0]
    device_keep = jnp.ones((local_heads,), jnp.float32)
    device_state = jnp.zeros((local_heads, head_dim, state_size), jnp.float32)
    parts = span_parts(values, b_half, c_half, steps_dt, decay_rates, segments, prev_first)
    device_keep = parts[3] * device_keep
    device_state = parts[3][:, None, None] * device_state + parts[2]
    identity = (jnp.ones_like(device_keep), jnp.zeros_like(device_state))
    prefix = prefix_2((device_keep, device_state), "seq", combine, identity)
    carried = prefix[1]
    intra_part, carry_in, fresh_state, keep_factor = parts
    inter_part = (
        jnp.einsum("in,hpn->ihp", c_rows, carried, precision=HIGHEST_PREC) * carry_in[:, :, None]
    )
    outputs = intra_part + inter_part
    mixed_heads = outputs + skip_gain[None, :, None] * values
    gated = mixed_heads.reshape(tokens_here, local_inner) * jax.nn.silu(
        gate_all.astype(jnp.float32)
    )
    squares = jnp.sum(gated * gated, axis=1)
    square_total = lax.psum(squares, "tp")
    mean_square = square_total / (local_inner * lax.axis_size("tp"))
    normed = (gated * lax.rsqrt(mean_square + EPSILON)[:, None] * norm_gain[None, :]).astype(
        jnp.bfloat16
    )
    out_weight = w_out.astype(jnp.bfloat16)
    partial_terms = jnp.dot(
        normed,
        lax.all_gather(out_weight, "seq", axis=1, tiled=True),
        preferred_element_type=jnp.float32,
    )
    return lax.psum_scatter(
        partial_terms.astype(jnp.bfloat16), "tp", scatter_dimension=1, tiled=True
    )


def place():
    seq, tp = lax.axis_index("seq"), lax.axis_index("tp")
    return seq, tp, seq // 2, seq % 2, tp // 2, tp % 2


def remote(src, dst, send, recv, seq, tp):
    return pltpu.make_async_remote_copy(
        src_ref=src, dst_ref=dst, send_sem=send, recv_sem=recv,
        device_id=(seq, tp), device_id_type=MESH,
    )


def greet(planes):
    seq, tp, z, x, y, c = place()
    barrier = pltpu.get_barrier_semaphore()

    def meet(to_seq, to_tp):
        pl.semaphore_signal(barrier, inc=1, device_id=(to_seq, to_tp), device_id_type=MESH)

    for other in range(1, 8):
        dx, dt = other // 4, other % 4
        meet(2 * z + (x + dx) % 2, (tp + dt) % 4)

    @pl.when(z > 0)
    def _():
        meet(seq - 2, tp)

        @pl.when(c == 0)
        def _():
            meet(seq - 2, tp + 1)

    @pl.when(z < planes - 1)
    def _():
        meet(seq + 2, tp)

        @pl.when(c == 1)
        def _():
            meet(seq + 2, tp - 1)

    below = jnp.where(z > 0, 2 - c, 0)
    above = jnp.where(z < planes - 1, 1 + c, 0)
    pl.semaphore_wait(barrier, 7 + below + above)


class Relay:
    def __init__(self, planes, depth, own, every, sems):
        self.planes, self.depth, self.own, self.every = planes, depth, own, every
        self.got, self.swapped, self.up, self.down, self.across = sems
        self.chunks = own.shape[0] // depth
        self.at = place()

    def rows(self, k):
        return pl.ds(pl.multiple_of(k * self.depth, self.depth), self.depth)

    def local(self, k):
        seq, tp, z, x, y, c = self.at
        return pltpu.make_async_copy(
            self.own.at[self.rows(k)], self.every.at[2 * z + c, self.rows(k)], self.got.at[2 * z + c, k]
        )

    def swap(self, k):
        seq, tp, z, x, y, c = self.at
        slot = 2 * z + 1 - c
        return remote(
            self.own.at[self.rows(k)], self.every.at[slot, self.rows(k)],
            self.swapped.at[k], self.got.at[slot, k], seq + 1 - 2 * x, tp + 1 - 2 * c,
        )

    def sent(self, slot, k, sems, to_seq, to_tp):
        here = self.every.at[slot, self.rows(k)]
        return remote(here, here, sems.at[slot // 2, k], self.got.at[slot, k], to_seq, to_tp)

    def going_up(self, slot, k):
        return self.sent(slot, k, self.up, self.at[0] + 2, self.at[1])

    def going_down(self, slot, k):
        return self.sent(slot, k, self.down, self.at[0] - 2, self.at[1])

    def going_across(self, slot, k):
        return self.sent(slot, k, self.across, self.at[0], self.at[1] + 1 - 2 * self.at[5])

    def start(self):
        seq, tp, z, x, y, c = self.at

        @pl.when(x == c)
        def _():
            @pl.loop(0, self.chunks)
            def _(k):
                self.local(k).start()

        @pl.when(x != c)
        def _():
            @pl.loop(0, self.chunks)
            def _(k):
                self.swap(k).start()

    def turn(self, far):
        seq, tp, z, x, y, c = self.at
        mine = 2 * z + c

        @pl.loop(0, self.chunks)
        def _(k):
            if far == 0:
                @pl.when(x == c)
                def _():
                    self.local(k).wait()

                @pl.when(x != c)
                def _():
                    self.going_across(mine, k).wait_recv()

                @pl.when(z < self.planes - 1)
                def _():
                    self.going_up(mine, k).start()

                @pl.when(z > 0)
                def _():
                    self.going_down(mine, k).start()

                self.going_across(mine, k).start()
            else:
                @pl.when(z >= far)
                def _():
                    slot = mine - 2 * far
                    self.going_across(slot, k).wait_recv()

                    @pl.when(z < self.planes - 1)
                    def _():
                        self.going_up(slot, k).start()

                    self.going_across(slot, k).start()

                @pl.when(z < self.planes - far)
                def _():
                    slot = mine + 2 * far
                    self.going_across(slot, k).wait_recv()

                    @pl.when(z > 0)
                    def _():
                        self.going_down(slot, k).start()

                    self.going_across(slot, k).start()

    def arrive(self, planes):
        c = self.at[5]

        @pl.loop(0, self.chunks)
        def _(k):
            for at in planes:
                self.going_across(2 * at + 1 - c, k).wait_recv()

    def leave(self):
        seq, tp, z, x, y, c = self.at

        @pl.loop(0, self.chunks)
        def _(k):
            for at in range(self.planes):
                slot = 2 * at + c
                self.going_across(slot, k).wait_send()

                @pl.when((z < self.planes - 1) & (z >= at))
                def _():
                    self.going_up(slot, k).wait_send()

                @pl.when((z > 0) & (z <= at))
                def _():
                    self.going_down(slot, k).wait_send()

            @pl.when(x != c)
            def _():
                self.swap(k).wait_send()


def mixer_kernel(
    planes, heads, inner_total,
    lengths_ref, order_ref, h_ref, gate_ref, value_ref, shared_ref, step_ref, taps_ref,
    shared_taps_ref, bias_ref, log_ref, skip_ref, gain_ref, w_out_ref, out_ref,
    w_own, w_all, o_own, o_all, acc, h_own, h_all, p_own, par, gates, rows_ext, edge_own, edge_got, mixed, part_own, part_got,
    fresh, state_got, state_own, leaving, arrived, sq_leaving, sq_arrived,
    w_got, w_swapped, w_up, w_down, w_across, o_got, o_swapped, o_up, o_down, o_across,
    h_send, h_got, p_sems, edge_sems, state_sems, part_sems, send, recv, sq_send, sq_recv,
):
    f32, bf16 = jnp.float32, jnp.bfloat16
    seq, tp, z, x, y, c = place()
    share = 2 * y + x
    first, last = (z == 0) & (c == 0), (z == planes - 1) & (c == 1)
    before = (seq - 2 * (1 - c), tp + 1 - 2 * c)
    after = (seq + 2 * c, tp + 1 - 2 * c)
    tokens, width = h_ref.shape[0], value_ref.shape[1]
    shared_width = shared_ref.shape[1]
    quarter = shared_width // 4
    mix_width, state_size, head_dim = width + 2 * quarter, shared_width // 2, width // heads
    half_features = h_ref.shape[1] // 2

    def quarter_of(array, which):
        total = jnp.zeros((array.shape[0], quarter), f32)
        for i in range(4):
            total = jnp.where(which == i, array[:, i * quarter : (i + 1) * quarter], total)
        return total

    w_own[:, 0:width] = value_ref[...].astype(bf16)
    lanes = lax.broadcasted_iota(jnp.int32, (heads, quarter), 1)
    pick = (lanes == lax.broadcasted_iota(jnp.int32, (heads, quarter), 0)).astype(f32).astype(bf16)
    steps = lax.dot_general(
        step_ref[...].astype(bf16), pick, (((0,), (0,)), ((), ())), preferred_element_type=f32
    )
    w_own[:, width:mix_width] = jnp.concatenate(
        [steps, quarter_of(shared_ref[...], tp)], axis=1
    ).astype(bf16)
    w_own[:, mix_width:] = gate_ref[...].astype(bf16)
    h_own[0] = h_ref[:, 0:half_features]
    h_own[1] = h_ref[:, half_features:]
    p_own[...] = jnp.zeros_like(p_own)
    p_own[0:4, :] = taps_ref[...]
    p_own[4:5, :] = gain_ref[...]
    p_own[5:6, 0:heads] = bias_ref[...]
    p_own[6:7, 0:heads] = log_ref[...]
    p_own[7:8, 0:heads] = skip_ref[...]
    greet(planes)

    into = Relay(planes, 48, w_own, w_all, (w_got, w_swapped, w_up, w_down, w_across))
    out_of = Relay(planes, 96, o_own, o_all, (o_got, o_swapped, o_up, o_down, o_across))
    par_local = pltpu.make_async_copy(p_own, par, p_sems.at[0])
    par_swap = remote(p_own, par, p_sems.at[1], p_sems.at[0], seq + 1 - 2 * x, tp + 1 - 2 * c)
    into.start()

    def features(to):
        return remote(
            h_own, h_all.at[pl.ds(2 * tp, 2)], h_send.at[to], h_got.at[tp],
            2 * z + to // 2, 2 * (to % 2) + x,
        )

    own_features = pltpu.make_async_copy(h_own, h_all.at[pl.ds(2 * tp, 2)], h_got.at[tp])
    for to in range(4):
        itself = (x == c) & (x == to // 2) & (y == to % 2)

        @pl.when(itself)
        def _():
            own_features.start()

        @pl.when(jnp.logical_not(itself))
        def _():
            features(to).start()

    @pl.when(x == c)
    def _():
        par_local.start()

    @pl.when(x != c)
    def _():
        par_swap.start()

    into.turn(0)
    o_own[...] = w_out_ref[...].astype(bf16)
    out_of.start()
    inside = (z > 0) & (z < planes - 1)
    outside = jnp.logical_not(inside)

    @pl.when(outside)
    def _():
        out_of.turn(0)

    for far in range(1, planes - 1):
        into.turn(far)

    @pl.when(inside)
    def _():
        out_of.turn(0)
        out_of.turn(1)

    for held in range(4):
        remote(
            h_own, h_all.at[pl.ds(2 * held, 2)], h_send.at[0], h_got.at[held],
            seq, tp + 1 - 2 * c,
        ).wait_recv()

    @pl.when(x == c)
    def _():
        par_local.wait()

    @pl.when(x != c)
    def _():
        par_swap.wait()

    nearest = [jnp.where(z < planes // 2, i, planes - 1 - i) for i in range(planes)]

    def project(start, size, part):
        total = jnp.zeros((tokens, size), f32)
        for plane in part:
            for block in (2 * plane, 2 * plane + 1):
                total = total + jnp.dot(
                    h_all[order_ref[block]], w_all[block, :, start : start + size],
                    preferred_element_type=f32,
                )
        return total

    into.arrive(nearest[:-1])
    for part in range(0, acc.shape[1], 384):
        size = min(384, acc.shape[1] - part)
        acc[:, part : part + size] = project(part, size, nearest[:-1])
    into.turn(planes - 1)
    into.arrive(nearest[-1:])

    def projected(start, size):
        return (acc[:, start : start + size] + project(start, size, nearest[-1:])).astype(bf16)

    for part in range(0, mix_width, 384):
        size = min(384, mix_width - part)
        done = projected(part, size)
        rows_ext[8:, part : part + size] = done.astype(f32)
        edge_own[:, part : part + size] = done[tokens - 16 :]

    def edge(to):
        return remote(edge_own, edge_got, edge_sems.at[0], edge_sems.at[1], *to)

    @pl.when(jnp.logical_not(last))
    def _():
        edge(after).start()

    gates[...] = projected(mix_width, width)
    raw = rows_ext[8:, width:mix_width]

    lane_heads = lax.broadcasted_iota(jnp.int32, (1, 128), 1) < heads
    bias = jnp.where(lane_heads, par[5:6, 0:128], 0.0)
    rate = jnp.where(lane_heads, jnp.exp(par[6:7, 0:128]), 0.0)
    shifted = raw + bias
    dt = jnp.maximum(shifted, 0.0) + jnp.log1p(jnp.exp(-jnp.abs(shifted)))
    row_at = lax.broadcasted_iota(jnp.int32, (tokens, tokens), 0)
    column_at = lax.broadcasted_iota(jnp.int32, (tokens, tokens), 1)
    first_pos = (2 * z + c) * tokens
    ends = [lengths_ref[0]]
    for i in range(1, lengths_ref.shape[0]):
        ends.append(ends[-1] + lengths_ref[i])

    def segment(position):
        count = jnp.zeros_like(position)
        for end in ends:
            count = count + (position >= end).astype(jnp.int32)
        return count

    row_segments, column_segments = segment(first_pos + row_at), segment(first_pos + column_at)
    causal = (row_at >= column_at) & (row_segments == column_segments)
    lower = (row_at >= column_at).astype(f32)
    summed = jnp.dot(lower, -dt * rate, precision=HIGHEST_PREC, preferred_element_type=f32)
    summed_rows, dt_rows = jnp.transpose(summed), jnp.transpose(dt)
    positions = first_pos + lax.broadcasted_iota(jnp.int32, (tokens, 128), 0)
    segments = segment(positions)
    prev_segment = segment(jnp.full((tokens, 128), first_pos - 1, jnp.int32))
    last_segment = segment(jnp.full((tokens, 128), first_pos + tokens - 1, jnp.int32))
    carry_in = jnp.where(segments == prev_segment, jnp.exp(summed), 0.0)
    end_sum = summed[tokens - 1 : tokens]
    tail = jnp.where(segments == last_segment, jnp.exp(end_sum - summed), 0.0) * dt
    keep = jnp.where(last_segment[0:8] == prev_segment[0:8], jnp.exp(end_sum), 0.0)
    spread = (
        lax.broadcasted_iota(jnp.int32, (128, width), 1) // head_dim
        == lax.broadcasted_iota(jnp.int32, (128, width), 0)
    ).astype(f32)

    def over_channels(per_head):
        return jnp.dot(per_head, spread, precision=HIGHEST_PREC, preferred_element_type=f32)

    keep_rows = lax.dot_general(
        spread, keep, (((0,), (1,)), ((), ())), precision=HIGHEST_PREC, preferred_element_type=f32
    )[:, 0:1]

    @pl.when(first)
    def _():
        rows_ext[0:8] = jnp.zeros((8, mix_width), f32)

    @pl.when(jnp.logical_not(first))
    def _():
        edge(before).wait_recv()
        rows_ext[0:8] = edge_got[...].astype(f32)[8:16]

    def convolve(start, size, taps):
        total = jnp.zeros((tokens, size), f32)
        for k in range(4):
            back = 3 - k
            counted = (segment(positions - back) == segments) & (positions >= back)
            term = taps[k : k + 1] * rows_ext[8 - back : 8 - back + tokens, start : start + size]
            total = total + jnp.where(counted[:, 0:1], term, 0.0)
        return jax.nn.silu(total).astype(bf16)

    shared_taps = quarter_of(shared_taps_ref[...], share)
    part_own[...] = convolve(
        width, 2 * quarter, jnp.concatenate([jnp.zeros_like(shared_taps), shared_taps], axis=1)
    )

    def piece(dx, dy):
        return remote(
            part_own, part_got.at[share], part_sems.at[0, 2 * dy + dx], part_sems.at[1, share],
            2 * z + (x + dx) % 2, 2 * ((y + dy) % 2) + c,
        )

    pieces = ((1, 1), (1, 0), (0, 1))
    for dx, dy in pieces:
        piece(dx, dy).start()
    part_got[share] = part_own[...]
    mixed[:, 0:width] = convolve(0, width, par[0:4])
    for dx, dy in pieces:
        source = 2 * ((y + dy) % 2) + (x + dx) % 2
        remote(
            part_own, part_got.at[source], part_sems.at[0, 0], part_sems.at[1, source],
            2 * z + (x + dx) % 2, 2 * ((y + dy) % 2) + c,
        ).wait_recv()
    for i in range(4):
        mixed[:, width + i * quarter : width + (i + 1) * quarter] = part_got[i][:, quarter:]
    values = mixed[:, 0:width]
    b_rows = mixed[:, width : width + state_size]
    c_rows = mixed[:, width + state_size :]
    weighted = (values.astype(f32) * over_channels(tail)).astype(bf16)
    fresh[...] = lax.dot_general(
        weighted, b_rows, (((0,), (0,)), ((), ())), preferred_element_type=f32
    )

    parts = 4
    depth = width // parts

    def state(part, to):
        at = pl.ds(part * depth, depth)
        return remote(
            state_own.at[at], state_got.at[at], state_sems.at[0, part], state_sems.at[1, part], *to
        )

    @pl.when(first)
    def _():
        state_got[...] = jnp.zeros_like(state_got)
        state_own[...] = fresh[...].astype(bf16)
        for part in range(parts):
            state(part, after).start()

    @pl.when(inside)
    def _():
        out_of.turn(2)

    @pl.when(outside)
    def _():
        out_of.turn(1)

    scores = lax.dot_general(c_rows, b_rows, (((1,), (1,)), ((), ())), preferred_element_type=f32)
    scores = jnp.where(causal, scores, 0.0)
    for head in range(heads):
        gap = summed[:, head : head + 1] - summed_rows[head : head + 1]
        weights = scores * jnp.exp(jnp.where(causal, gap, 0.0)) * dt_rows[head : head + 1]
        at = slice(head * head_dim, (head + 1) * head_dim)
        rows_ext[8:, at] = jnp.dot(
            weights.astype(bf16), mixed[:, at], preferred_element_type=f32
        )

    @pl.when(jnp.logical_not(first))
    def _():
        for part in range(parts):
            state(part, before).wait_recv()

            @pl.when(jnp.logical_not(last))
            def _():
                at = slice(part * depth, (part + 1) * depth)
                state_own[at] = (
                    keep_rows[at] * state_got[at].astype(f32) + fresh[at]
                ).astype(bf16)
                state(part, after).start()

    @pl.when(outside)
    def _():
        for far in range(2, planes - 1):
            out_of.turn(far)

    inter = lax.dot_general(
        c_rows, state_got[...], (((1,), (1,)), ((), ())), preferred_element_type=f32
    ) * over_channels(carry_in)
    skip = over_channels(
        jnp.broadcast_to(jnp.where(lane_heads, par[7:8, 0:128], 0.0), (8, 128))
    )[0:1]
    gated = (rows_ext[8:, 0:width] + inter + skip * values.astype(f32)) * jax.nn.silu(
        gates[...].astype(f32)
    )
    sums = lax.dot_general(
        jnp.ones((8, width), f32), gated * gated, (((1,), (1,)), ((), ())),
        precision=HIGHEST_PREC, preferred_element_type=f32,
    )
    sq_leaving[...] = sums
    scaled = (gated * par[4:5]).astype(bf16)
    columns = 2 * w_out_ref.shape[0]

    def outward(to):
        return remote(leaving.at[to], arrived.at[share], send.at[to], recv.at[share], 2 * z + c, to)

    def squares(to):
        return remote(
            sq_leaving, sq_arrived.at[share], sq_send.at[to], sq_recv.at[share], 2 * z + c, to
        )

    for to in nearest:
        if to is nearest[-1]:
            @pl.when(outside)
            def _():
                out_of.turn(planes - 1)

        out_of.arrive([to])
        product = lax.dot_general(
            scaled, o_all[pl.ds(2 * to, 2)].reshape(columns, width),
            (((1,), (1,)), ((), ())), preferred_element_type=f32,
        ).astype(bf16)
        itself = (x == c) & (tp == to)

        @pl.when(itself)
        def _():
            arrived[share] = product
            sq_arrived[share] = sums

        @pl.when(jnp.logical_not(itself))
        def _(to=to, product=product):
            leaving[to] = product
            outward(to).start()
            squares(to).start()

    into.leave()
    for dx, dy in pieces:
        piece(dx, dy).wait_send()
    out_of.leave()
    for to in range(4):
        itself = (x == c) & (x == to // 2) & (y == to % 2)

        @pl.when(jnp.logical_not(itself))
        def _():
            features(to).wait_send()

    @pl.when(jnp.logical_not(last))
    def _():
        edge(after).wait_send()
        for part in range(parts):
            state(part, after).wait_send()

    total, sq_total = 0.0, 0.0
    for slot in range(4):
        @pl.when(jnp.logical_not((x == c) & (share == slot)))
        def _():
            remote(
                leaving.at[0], arrived.at[slot], send.at[0], recv.at[slot], seq, tp + 1 - 2 * c
            ).wait_recv()
            remote(
                sq_leaving, sq_arrived.at[slot], sq_send.at[0], sq_recv.at[slot],
                seq, tp + 1 - 2 * c,
            ).wait_recv()

        total = total + arrived[slot].astype(f32)
        sq_total = sq_total + sq_arrived[slot]
    scale = lax.rsqrt(sq_total[0:1] / inner_total + EPSILON)
    scale_rows = jnp.transpose(jnp.broadcast_to(scale, (128, tokens)))[:, 0:1]
    out_ref[...] = (total * scale_rows).astype(out_ref.dtype)

    for to in range(4):
        itself = (x == c) & (tp == to)

        @pl.when(jnp.logical_not(itself))
        def _():
            outward(to).wait_send()
            squares(to).wait_send()


def on_device_paired(
    hidden_in,
    w_in_gate,
    w_in_value,
    w_in_shared,
    w_in_step,
    conv_value,
    conv_shared,
    dt_bias,
    a_log,
    skip_gain,
    norm_gain,
    w_out,
    prompt_lengths,
    row_blocks,
):
    blocks = lax.axis_size("seq")
    planes = blocks // 2
    tokens, features = hidden_in.shape
    rows, width = w_in_value.shape
    shared_width, heads = w_in_shared.shape[1], dt_bias.shape[0]
    mix_width = width + shared_width // 2
    in_width = mix_width + width
    state_size = shared_width // 2
    out_columns = w_out.shape[1]
    f32, bf16, dma = jnp.float32, jnp.bfloat16, pltpu.SemaphoreType.DMA
    vmem, smem = pl.BlockSpec(memory_space=pltpu.VMEM), pl.BlockSpec(memory_space=pltpu.SMEM)

    def relay_sems(chunks):
        return [dma((blocks, chunks)), dma((chunks,))] + [dma((planes, chunks))] * 3

    return pl.pallas_call(
        functools.partial(mixer_kernel, planes, heads, width * lax.axis_size("tp")),
        out_shape=jax.ShapeDtypeStruct((tokens, features), bf16),
        in_specs=[smem] * 2 + [vmem] * 12,
        out_specs=vmem,
        scratch_shapes=[
            pltpu.VMEM((rows, in_width), bf16),
            pltpu.VMEM((blocks, rows, in_width), bf16),
            pltpu.VMEM((out_columns, width), bf16),
            pltpu.VMEM((blocks, out_columns, width), bf16),
            pltpu.VMEM((tokens, in_width), f32),
            pltpu.VMEM((2, tokens, features // 2), bf16),
            pltpu.VMEM((8, tokens, features // 2), bf16),
            pltpu.VMEM((8, width), f32),
            pltpu.VMEM((8, width), f32),
            pltpu.VMEM((tokens, width), bf16),
            pltpu.VMEM((tokens + 8, mix_width), f32),
            pltpu.VMEM((16, mix_width), bf16),
            pltpu.VMEM((16, mix_width), bf16),
            pltpu.VMEM((tokens, width + shared_width), bf16),
            pltpu.VMEM((tokens, shared_width // 2), bf16),
            pltpu.VMEM((4, tokens, shared_width // 2), bf16),
            pltpu.VMEM((width, state_size), f32),
            pltpu.VMEM((width, state_size), bf16),
            pltpu.VMEM((width, state_size), bf16),
            pltpu.VMEM((4, tokens, features), bf16),
            pltpu.VMEM((4, tokens, features), bf16),
            pltpu.VMEM((8, tokens), f32),
            pltpu.VMEM((4, 8, tokens), f32),
        ]
        + relay_sems(rows // 48)
        + relay_sems(out_columns // 96)
        + [dma((4,)), dma((4,)), dma((2,)), dma((2,)), dma((2, 4)), dma((2, 4))]
        + [dma((4,))] * 4,
        compiler_params=pltpu.CompilerParams(
            collective_id=0, has_side_effects=True, vmem_limit_bytes=50 << 20
        ),
        name="mixer",
    )(
        prompt_lengths,
        row_blocks,
        hidden_in,
        w_in_gate,
        w_in_value,
        w_in_shared,
        w_in_step.T,
        conv_value,
        conv_shared,
        dt_bias[None],
        a_log[None],
        skip_gain[None],
        norm_gain[None],
        w_out.T,
    )


def paired(mesh):
    return dict(mesh.shape) == {"seq": 8, "tp": 4}


def solution(mesh):
    return jax.shard_map(
        on_device_paired if paired(mesh) else on_device_plain,
        mesh=mesh,
        in_specs=(
            P("seq", "tp"),
            P("seq", "tp"),
            P("seq", "tp"),
            P("seq", None),
            P("seq", "tp"),
            P(None, "tp"),
            P(),
            P("tp"),
            P("tp"),
            P("tp"),
            P("tp"),
            P("tp", "seq"),
            P(),
            P(),
        ),
        out_specs=P("seq", "tp"),
        check_vma=False,
    )
```

```python
import functools

import jax
import jax.numpy as jnp
from jax import lax
from jax.experimental import pallas as pl
from jax.experimental.pallas import tpu as pltpu
from jax.sharding import PartitionSpec as P

MESH = pl.DeviceIdType.MESH

EPSILON = 1e-05
HIGHEST_PREC = lax.Precision.HIGHEST


def passed_along(block, axis, distance):
    devices = range(lax.axis_size(axis))
    route = [(i - distance, i) for i in devices if i - distance in devices]
    return lax.ppermute(block, axis, route)


def prefix_2(x, axis, combine, identity):
    count, here = (lax.axis_size(axis), lax.axis_index(axis))
    everything = jax.tree.map(
        lambda part, kind: lax.all_gather(part.astype(kind), axis), x, (jnp.bfloat16, jnp.bfloat16)
    )
    start = jax.tree.map(
        lambda part, zero: jnp.broadcast_to(jnp.asarray(zero, part.dtype), part.shape), x, identity
    )

    def turn(k, before):
        reached = k < here
        new = combine(
            before, jax.tree.map(lambda part, own: part[k].astype(own.dtype), everything, x)
        )
        return jax.tree.map(lambda a, b: jnp.where(reached, a, b), new, before)

    return lax.fori_loop(0, count, turn, start)


def segment_of(positions, doc_ends):
    return jnp.sum((positions[:, None] >= doc_ends[None, :]).astype(jnp.int32), axis=1)


def span_parts(values, b_half, c_half, steps_dt, decay_rates, segments, prev_seg):
    length = values.shape[0]
    b_rows = b_half.astype(jnp.float32)
    cumulative = jnp.cumsum(-steps_dt * decay_rates[None, :], axis=0)
    places = jnp.arange(length)
    causal = (places[:, None] >= places[None, :]) & (segments[:, None] == segments[None, :])
    gaps_log = jnp.where(causal[:, :, None], cumulative[:, None, :] - cumulative[None, :, :], 0.0)
    decays_in = jnp.where(causal[:, :, None], jnp.exp(gaps_log), 0.0)
    scores = jnp.dot(c_half, b_half.T, preferred_element_type=jnp.float32)
    weights = scores[:, :, None] * decays_in * steps_dt[None, :, :]
    intra_part = jnp.einsum("ijh,jhp->ihp", weights, values, precision=HIGHEST_PREC)
    carry_in = jnp.where((segments == prev_seg)[:, None], jnp.exp(cumulative), 0.0)
    tail_weight = (
        jnp.where(
            (segments == segments[-1])[:, None], jnp.exp(cumulative[-1][None, :] - cumulative), 0.0
        )
        * steps_dt
    )
    fresh_state = jnp.einsum("jh,jhp,jn->hpn", tail_weight, values, b_rows, precision=HIGHEST_PREC)
    keep_factor = jnp.where(segments[-1] == prev_seg, jnp.exp(cumulative[-1]), 0.0)
    return (intra_part, carry_in, fresh_state, keep_factor)


def combine(earlier, later):
    return (earlier[0] * later[0], later[0][:, None, None] * earlier[1] + later[1])


def on_device_plain(
    hidden_in,
    w_in_gate,
    w_in_value,
    w_in_shared,
    w_in_step,
    conv_value,
    conv_shared,
    dt_bias,
    a_log,
    skip_gain,
    norm_gain,
    w_out,
    prompt_lengths,
    row_blocks,
):
    seq_count = lax.axis_size("seq")
    tokens_here = hidden_in.shape[0]
    edge_count = conv_value.shape[0] - 1
    gathered = lax.all_gather(hidden_in, "tp", axis=1, tiled=True)
    row_count = gathered.shape[0]
    model_width = gathered.shape[1]
    permuted = jnp.take(
        gathered.reshape(row_count, seq_count, model_width // seq_count), row_blocks, axis=1
    ).reshape(row_count, model_width)
    stored = (
        w_in_gate.astype(jnp.bfloat16),
        w_in_value.astype(jnp.bfloat16),
        w_in_shared.astype(jnp.bfloat16),
        w_in_step.astype(jnp.bfloat16),
    )
    pieces = (
        lax.all_gather(stored[0], "seq", axis=0, tiled=True),
        lax.all_gather(stored[1], "seq", axis=0, tiled=True),
        lax.all_gather(stored[2], "seq", axis=0, tiled=True),
        lax.all_gather(stored[3], "seq", axis=0, tiled=True),
    )
    projected = tuple(
        (
            jnp.dot(permuted, weight_piece, preferred_element_type=jnp.float32)
            for weight_piece in pieces
        )
    )
    gate_all, value_all, shared_all, raw_all = [result.astype(jnp.bfloat16) for result in projected]
    mixed_in = jnp.concatenate([value_all, shared_all], axis=1)
    edge_mix = passed_along(mixed_in[tokens_here - edge_count :], "seq", 1)
    doc_ends = jnp.cumsum(prompt_lengths)
    first_pos = lax.axis_index("seq") * tokens_here
    positions = first_pos + jnp.arange(tokens_here, dtype=jnp.int32)
    edge_positions = first_pos - edge_count + jnp.arange(edge_count, dtype=jnp.int32)
    segments = segment_of(positions, doc_ends)
    ext_segments = jnp.concatenate([segment_of(edge_positions, doc_ends), segments])
    ext_rows = jnp.concatenate([edge_mix, mixed_in], axis=0)
    kernel = jnp.concatenate([conv_value, conv_shared], axis=1)
    conv_sum = jnp.zeros(mixed_in.shape, jnp.float32)
    for tap_index in range(edge_count + 1):
        same_doc = (ext_segments[tap_index : tap_index + tokens_here] == segments)[:, None]
        conv_sum = conv_sum + jnp.where(
            same_doc,
            kernel[tap_index][None, :]
            * ext_rows[tap_index : tap_index + tokens_here].astype(jnp.float32),
            0.0,
        )
    convolved = jax.nn.silu(conv_sum).astype(jnp.bfloat16)
    local_inner = conv_value.shape[1]
    local_heads = dt_bias.shape[0]
    head_dim = local_inner // local_heads
    state_size = conv_shared.shape[1] // 2
    values = (
        convolved[:, :local_inner].astype(jnp.float32).reshape(tokens_here, local_heads, head_dim)
    )
    b_half = convolved[:, local_inner : local_inner + state_size]
    c_half = convolved[:, local_inner + state_size :]
    c_rows = c_half.astype(jnp.float32)
    steps_dt = jax.nn.softplus(raw_all.astype(jnp.float32) + dt_bias[None, :])
    decay_rates = jnp.exp(a_log)
    prev_first = segment_of(jnp.reshape(first_pos - 1, (1,)), doc_ends)[0]
    device_keep = jnp.ones((local_heads,), jnp.float32)
    device_state = jnp.zeros((local_heads, head_dim, state_size), jnp.float32)
    parts = span_parts(values, b_half, c_half, steps_dt, decay_rates, segments, prev_first)
    device_keep = parts[3] * device_keep
    device_state = parts[3][:, None, None] * device_state + parts[2]
    identity = (jnp.ones_like(device_keep), jnp.zeros_like(device_state))
    prefix = prefix_2((device_keep, device_state), "seq", combine, identity)
    carried = prefix[1]
    intra_part, carry_in, fresh_state, keep_factor = parts
    inter_part = (
        jnp.einsum("in,hpn->ihp", c_rows, carried, precision=HIGHEST_PREC) * carry_in[:, :, None]
    )
    outputs = intra_part + inter_part
    mixed_heads = outputs + skip_gain[None, :, None] * values
    gated = mixed_heads.reshape(tokens_here, local_inner) * jax.nn.silu(
        gate_all.astype(jnp.float32)
    )
    squares = jnp.sum(gated * gated, axis=1)
    square_total = lax.psum(squares, "tp")
    mean_square = square_total / (local_inner * lax.axis_size("tp"))
    normed = (gated * lax.rsqrt(mean_square + EPSILON)[:, None] * norm_gain[None, :]).astype(
        jnp.bfloat16
    )
    out_weight = w_out.astype(jnp.bfloat16)
    partial_terms = jnp.dot(
        normed,
        lax.all_gather(out_weight, "seq", axis=1, tiled=True),
        preferred_element_type=jnp.float32,
    )
    return lax.psum_scatter(
        partial_terms.astype(jnp.bfloat16), "tp", scatter_dimension=1, tiled=True
    )


def place():
    seq, tp = lax.axis_index("seq"), lax.axis_index("tp")
    return seq, tp, seq // 2, seq % 2, tp // 2, tp % 2


def remote(src, dst, send, recv, seq, tp):
    return pltpu.make_async_remote_copy(
        src_ref=src, dst_ref=dst, send_sem=send, recv_sem=recv,
        device_id=(seq, tp), device_id_type=MESH,
    )


def greet(planes):
    seq, tp, z, x, y, c = place()
    barrier = pltpu.get_barrier_semaphore()

    def meet(to_seq, to_tp):
        pl.semaphore_signal(barrier, inc=1, device_id=(to_seq, to_tp), device_id_type=MESH)

    for other in range(1, 8):
        dx, dt = other // 4, other % 4
        meet(2 * z + (x + dx) % 2, (tp + dt) % 4)

    @pl.when(z > 0)
    def _():
        meet(seq - 2, tp)

        @pl.when(c == 0)
        def _():
            meet(seq - 2, tp + 1)

    @pl.when(z < planes - 1)
    def _():
        meet(seq + 2, tp)

        @pl.when(c == 1)
        def _():
            meet(seq + 2, tp - 1)

    below = jnp.where(z > 0, 2 - c, 0)
    above = jnp.where(z < planes - 1, 1 + c, 0)
    pl.semaphore_wait(barrier, 7 + below + above)


class Relay:
    def __init__(self, planes, depth, own, every, sems):
        self.planes, self.depth, self.own, self.every = planes, depth, own, every
        self.got, self.swapped, self.up, self.down, self.across = sems
        self.chunks = own.shape[0] // depth
        self.at = place()

    def rows(self, k):
        return pl.ds(pl.multiple_of(k * self.depth, self.depth), self.depth)

    def local(self, k):
        seq, tp, z, x, y, c = self.at
        return pltpu.make_async_copy(
            self.own.at[self.rows(k)], self.every.at[2 * z + c, self.rows(k)], self.got.at[2 * z + c, k]
        )

    def swap(self, k):
        seq, tp, z, x, y, c = self.at
        slot = 2 * z + 1 - c
        return remote(
            self.own.at[self.rows(k)], self.every.at[slot, self.rows(k)],
            self.swapped.at[k], self.got.at[slot, k], seq + 1 - 2 * x, tp + 1 - 2 * c,
        )

    def sent(self, slot, k, sems, to_seq, to_tp):
        here = self.every.at[slot, self.rows(k)]
        return remote(here, here, sems.at[slot // 2, k], self.got.at[slot, k], to_seq, to_tp)

    def going_up(self, slot, k):
        return self.sent(slot, k, self.up, self.at[0] + 2, self.at[1])

    def going_down(self, slot, k):
        return self.sent(slot, k, self.down, self.at[0] - 2, self.at[1])

    def going_across(self, slot, k):
        return self.sent(slot, k, self.across, self.at[0], self.at[1] + 1 - 2 * self.at[5])

    def start(self):
        seq, tp, z, x, y, c = self.at

        @pl.when(x == c)
        def _():
            @pl.loop(0, self.chunks)
            def _(k):
                self.local(k).start()

        @pl.when(x != c)
        def _():
            @pl.loop(0, self.chunks)
            def _(k):
                self.swap(k).start()

    def turn(self, far):
        seq, tp, z, x, y, c = self.at
        mine = 2 * z + c

        @pl.loop(0, self.chunks)
        def _(k):
            if far == 0:
                @pl.when(x == c)
                def _():
                    self.local(k).wait()

                @pl.when(x != c)
                def _():
                    self.going_across(mine, k).wait_recv()

                @pl.when(z < self.planes - 1)
                def _():
                    self.going_up(mine, k).start()

                @pl.when(z > 0)
                def _():
                    self.going_down(mine, k).start()

                self.going_across(mine, k).start()
            else:
                @pl.when(z >= far)
                def _():
                    slot = mine - 2 * far
                    self.going_across(slot, k).wait_recv()

                    @pl.when(z < self.planes - 1)
                    def _():
                        self.going_up(slot, k).start()

                    self.going_across(slot, k).start()

                @pl.when(z < self.planes - far)
                def _():
                    slot = mine + 2 * far
                    self.going_across(slot, k).wait_recv()

                    @pl.when(z > 0)
                    def _():
                        self.going_down(slot, k).start()

                    self.going_across(slot, k).start()

    def arrive(self, planes):
        c = self.at[5]

        @pl.loop(0, self.chunks)
        def _(k):
            for at in planes:
                self.going_across(2 * at + 1 - c, k).wait_recv()

    def leave(self):
        seq, tp, z, x, y, c = self.at

        @pl.loop(0, self.chunks)
        def _(k):
            for at in range(self.planes):
                slot = 2 * at + c
                self.going_across(slot, k).wait_send()

                @pl.when((z < self.planes - 1) & (z >= at))
                def _():
                    self.going_up(slot, k).wait_send()

                @pl.when((z > 0) & (z <= at))
                def _():
                    self.going_down(slot, k).wait_send()

            @pl.when(x != c)
            def _():
                self.swap(k).wait_send()


def mixer_kernel(
    planes, heads, inner_total,
    lengths_ref, order_ref, *refs,
):
    arguments, (out_ref, *held) = refs[:12], refs[12:]
    inside_refs, (load_sems, *scratch) = held[:12], held[12:]
    (
        h_ref, gate_ref, value_ref, shared_ref, step_ref, taps_ref,
        shared_taps_ref, bias_ref, log_ref, skip_ref, gain_ref, w_out_ref,
    ) = inside_refs
    (
        w_own, w_all, o_own, o_all, acc, h_own, h_all, p_own, par, gates, rows_ext, edge_own, edge_got, mixed, part_own, part_got,
    fresh, state_got, state_own, leaving, arrived, sq_leaving, sq_arrived,
    w_got, w_swapped, w_up, w_down, w_across, o_got, o_swapped, o_up, o_down, o_across,
    h_send, h_got, p_sems, edge_sems, state_sems, part_sems, send, recv, sq_send, sq_recv,
    ) = scratch
    loads = [
        pltpu.make_async_copy(argument, inside, load_sems.at[i])
        for i, (argument, inside) in enumerate(zip(arguments, inside_refs))
    ]
    for load in loads:
        load.start()
    greet(planes)
    for load in loads:
        load.wait()
    f32, bf16 = jnp.float32, jnp.bfloat16
    seq, tp, z, x, y, c = place()
    share = 2 * y + x
    first, last = (z == 0) & (c == 0), (z == planes - 1) & (c == 1)
    before = (seq - 2 * (1 - c), tp + 1 - 2 * c)
    after = (seq + 2 * c, tp + 1 - 2 * c)
    tokens, width = h_ref.shape[0], value_ref.shape[1]
    shared_width = shared_ref.shape[1]
    quarter = shared_width // 4
    mix_width, state_size, head_dim = width + 2 * quarter, shared_width // 2, width // heads
    half_features = h_ref.shape[1] // 2

    def quarter_of(array, which):
        total = jnp.zeros((array.shape[0], quarter), f32)
        for i in range(4):
            total = jnp.where(which == i, array[:, i * quarter : (i + 1) * quarter], total)
        return total

    w_own[:, 0:width] = value_ref[...].astype(bf16)
    lanes = lax.broadcasted_iota(jnp.int32, (heads, quarter), 1)
    pick = (lanes == lax.broadcasted_iota(jnp.int32, (heads, quarter), 0)).astype(f32).astype(bf16)
    steps = lax.dot_general(
        step_ref[...].astype(bf16), pick, (((0,), (0,)), ((), ())), preferred_element_type=f32
    )
    w_own[:, width:mix_width] = jnp.concatenate(
        [steps, quarter_of(shared_ref[...], tp)], axis=1
    ).astype(bf16)
    w_own[:, mix_width:] = gate_ref[...].astype(bf16)
    h_own[0] = h_ref[:, 0:half_features]
    h_own[1] = h_ref[:, half_features:]
    p_own[...] = jnp.zeros_like(p_own)
    p_own[0:4, :] = taps_ref[...]
    p_own[4:5, :] = gain_ref[...]
    p_own[5:6, 0:heads] = bias_ref[...]
    p_own[6:7, 0:heads] = log_ref[...]
    p_own[7:8, 0:heads] = skip_ref[...]

    into = Relay(planes, 48, w_own, w_all, (w_got, w_swapped, w_up, w_down, w_across))
    out_of = Relay(planes, 96, o_own, o_all, (o_got, o_swapped, o_up, o_down, o_across))
    par_local = pltpu.make_async_copy(p_own, par, p_sems.at[0])
    par_swap = remote(p_own, par, p_sems.at[1], p_sems.at[0], seq + 1 - 2 * x, tp + 1 - 2 * c)
    into.start()

    def features(to):
        return remote(
            h_own, h_all.at[pl.ds(2 * tp, 2)], h_send.at[to], h_got.at[tp],
            2 * z + to // 2, 2 * (to % 2) + x,
        )

    own_features = pltpu.make_async_copy(h_own, h_all.at[pl.ds(2 * tp, 2)], h_got.at[tp])
    for to in range(4):
        itself = (x == c) & (x == to // 2) & (y == to % 2)

        @pl.when(itself)
        def _():
            own_features.start()

        @pl.when(jnp.logical_not(itself))
        def _():
            features(to).start()

    @pl.when(x == c)
    def _():
        par_local.start()

    @pl.when(x != c)
    def _():
        par_swap.start()

    into.turn(0)
    o_own[...] = w_out_ref[...].astype(bf16)
    out_of.start()
    inside = (z > 0) & (z < planes - 1)
    outside = jnp.logical_not(inside)

    @pl.when(outside)
    def _():
        out_of.turn(0)

    for far in range(1, planes - 1):
        into.turn(far)

    @pl.when(inside)
    def _():
        out_of.turn(0)
        out_of.turn(1)

    for held in range(4):
        remote(
            h_own, h_all.at[pl.ds(2 * held, 2)], h_send.at[0], h_got.at[held],
            seq, tp + 1 - 2 * c,
        ).wait_recv()

    @pl.when(x == c)
    def _():
        par_local.wait()

    @pl.when(x != c)
    def _():
        par_swap.wait()

    nearest = [jnp.where(z < planes // 2, i, planes - 1 - i) for i in range(planes)]

    def project(start, size, part):
        total = jnp.zeros((tokens, size), f32)
        for plane in part:
            for block in (2 * plane, 2 * plane + 1):
                total = total + jnp.dot(
                    h_all[order_ref[block]], w_all[block, :, start : start + size],
                    preferred_element_type=f32,
                )
        return total

    into.arrive(nearest[:-1])
    for part in range(0, acc.shape[1], 384):
        size = min(384, acc.shape[1] - part)
        acc[:, part : part + size] = project(part, size, nearest[:-1])
    into.turn(planes - 1)
    into.arrive(nearest[-1:])

    def projected(start, size):
        return (acc[:, start : start + size] + project(start, size, nearest[-1:])).astype(bf16)

    for part in range(0, mix_width, 384):
        size = min(384, mix_width - part)
        done = projected(part, size)
        rows_ext[8:, part : part + size] = done.astype(f32)
        edge_own[:, part : part + size] = done[tokens - 16 :]

    def edge(to):
        return remote(edge_own, edge_got, edge_sems.at[0], edge_sems.at[1], *to)

    @pl.when(jnp.logical_not(last))
    def _():
        edge(after).start()

    gates[...] = projected(mix_width, width)
    raw = rows_ext[8:, width:mix_width]

    lane_heads = lax.broadcasted_iota(jnp.int32, (1, 128), 1) < heads
    bias = jnp.where(lane_heads, par[5:6, 0:128], 0.0)
    rate = jnp.where(lane_heads, jnp.exp(par[6:7, 0:128]), 0.0)
    shifted = raw + bias
    dt = jnp.maximum(shifted, 0.0) + jnp.log1p(jnp.exp(-jnp.abs(shifted)))
    row_at = lax.broadcasted_iota(jnp.int32, (tokens, tokens), 0)
    column_at = lax.broadcasted_iota(jnp.int32, (tokens, tokens), 1)
    first_pos = (2 * z + c) * tokens
    ends = [lengths_ref[0]]
    for i in range(1, lengths_ref.shape[0]):
        ends.append(ends[-1] + lengths_ref[i])

    def segment(position):
        count = jnp.zeros_like(position)
        for end in ends:
            count = count + (position >= end).astype(jnp.int32)
        return count

    row_segments, column_segments = segment(first_pos + row_at), segment(first_pos + column_at)
    causal = (row_at >= column_at) & (row_segments == column_segments)
    lower = (row_at >= column_at).astype(f32)
    summed = jnp.dot(lower, -dt * rate, precision=HIGHEST_PREC, preferred_element_type=f32)
    summed_rows, dt_rows = jnp.transpose(summed), jnp.transpose(dt)
    positions = first_pos + lax.broadcasted_iota(jnp.int32, (tokens, 128), 0)
    segments = segment(positions)
    prev_segment = segment(jnp.full((tokens, 128), first_pos - 1, jnp.int32))
    last_segment = segment(jnp.full((tokens, 128), first_pos + tokens - 1, jnp.int32))
    carry_in = jnp.where(segments == prev_segment, jnp.exp(summed), 0.0)
    end_sum = summed[tokens - 1 : tokens]
    tail = jnp.where(segments == last_segment, jnp.exp(end_sum - summed), 0.0) * dt
    keep = jnp.where(last_segment[0:8] == prev_segment[0:8], jnp.exp(end_sum), 0.0)
    spread = (
        lax.broadcasted_iota(jnp.int32, (128, width), 1) // head_dim
        == lax.broadcasted_iota(jnp.int32, (128, width), 0)
    ).astype(f32)

    def over_channels(per_head):
        return jnp.dot(per_head, spread, precision=HIGHEST_PREC, preferred_element_type=f32)

    keep_rows = lax.dot_general(
        spread, keep, (((0,), (1,)), ((), ())), precision=HIGHEST_PREC, preferred_element_type=f32
    )[:, 0:1]

    @pl.when(first)
    def _():
        rows_ext[0:8] = jnp.zeros((8, mix_width), f32)

    @pl.when(jnp.logical_not(first))
    def _():
        edge(before).wait_recv()
        rows_ext[0:8] = edge_got[...].astype(f32)[8:16]

    def convolve(start, size, taps):
        total = jnp.zeros((tokens, size), f32)
        for k in range(4):
            back = 3 - k
            counted = (segment(positions - back) == segments) & (positions >= back)
            term = taps[k : k + 1] * rows_ext[8 - back : 8 - back + tokens, start : start + size]
            total = total + jnp.where(counted[:, 0:1], term, 0.0)
        return jax.nn.silu(total).astype(bf16)

    shared_taps = quarter_of(shared_taps_ref[...], share)
    part_own[...] = convolve(
        width, 2 * quarter, jnp.concatenate([jnp.zeros_like(shared_taps), shared_taps], axis=1)
    )

    def piece(dx, dy):
        return remote(
            part_own, part_got.at[share], part_sems.at[0, 2 * dy + dx], part_sems.at[1, share],
            2 * z + (x + dx) % 2, 2 * ((y + dy) % 2) + c,
        )

    pieces = ((1, 1), (1, 0), (0, 1))
    for dx, dy in pieces:
        piece(dx, dy).start()
    part_got[share] = part_own[...]
    mixed[:, 0:width] = convolve(0, width, par[0:4])
    for dx, dy in pieces:
        source = 2 * ((y + dy) % 2) + (x + dx) % 2
        remote(
            part_own, part_got.at[source], part_sems.at[0, 0], part_sems.at[1, source],
            2 * z + (x + dx) % 2, 2 * ((y + dy) % 2) + c,
        ).wait_recv()
    for i in range(4):
        mixed[:, width + i * quarter : width + (i + 1) * quarter] = part_got[i][:, quarter:]
    values = mixed[:, 0:width]
    b_rows = mixed[:, width : width + state_size]
    c_rows = mixed[:, width + state_size :]
    weighted = (values.astype(f32) * over_channels(tail)).astype(bf16)
    fresh[...] = lax.dot_general(
        weighted, b_rows, (((0,), (0,)), ((), ())), preferred_element_type=f32
    )

    parts = 4
    depth = width // parts

    def state(part, to):
        at = pl.ds(part * depth, depth)
        return remote(
            state_own.at[at], state_got.at[at], state_sems.at[0, part], state_sems.at[1, part], *to
        )

    @pl.when(first)
    def _():
        state_got[...] = jnp.zeros_like(state_got)
        state_own[...] = fresh[...].astype(bf16)
        for part in range(parts):
            state(part, after).start()

    @pl.when(inside)
    def _():
        out_of.turn(2)

    @pl.when(outside)
    def _():
        out_of.turn(1)

    scores = lax.dot_general(c_rows, b_rows, (((1,), (1,)), ((), ())), preferred_element_type=f32)
    scores = jnp.where(causal, scores, 0.0)
    for head in range(heads):
        gap = summed[:, head : head + 1] - summed_rows[head : head + 1]
        weights = scores * jnp.exp(jnp.where(causal, gap, 0.0)) * dt_rows[head : head + 1]
        at = slice(head * head_dim, (head + 1) * head_dim)
        rows_ext[8:, at] = jnp.dot(
            weights.astype(bf16), mixed[:, at], preferred_element_type=f32
        )

    @pl.when(jnp.logical_not(first))
    def _():
        for part in range(parts):
            state(part, before).wait_recv()

            @pl.when(jnp.logical_not(last))
            def _():
                at = slice(part * depth, (part + 1) * depth)
                state_own[at] = (
                    keep_rows[at] * state_got[at].astype(f32) + fresh[at]
                ).astype(bf16)
                state(part, after).start()

    @pl.when(outside)
    def _():
        for far in range(2, planes - 1):
            out_of.turn(far)

    inter = lax.dot_general(
        c_rows, state_got[...], (((1,), (1,)), ((), ())), preferred_element_type=f32
    ) * over_channels(carry_in)
    skip = over_channels(
        jnp.broadcast_to(jnp.where(lane_heads, par[7:8, 0:128], 0.0), (8, 128))
    )[0:1]
    gated = (rows_ext[8:, 0:width] + inter + skip * values.astype(f32)) * jax.nn.silu(
        gates[...].astype(f32)
    )
    sums = lax.dot_general(
        jnp.ones((8, width), f32), gated * gated, (((1,), (1,)), ((), ())),
        precision=HIGHEST_PREC, preferred_element_type=f32,
    )
    sq_leaving[...] = sums
    scaled = (gated * par[4:5]).astype(bf16)
    columns = 2 * w_out_ref.shape[0]

    def outward(to):
        return remote(leaving.at[to], arrived.at[share], send.at[to], recv.at[share], 2 * z + c, to)

    def squares(to):
        return remote(
            sq_leaving, sq_arrived.at[share], sq_send.at[to], sq_recv.at[share], 2 * z + c, to
        )

    for to in nearest:
        if to is nearest[-1]:
            @pl.when(outside)
            def _():
                out_of.turn(planes - 1)

        out_of.arrive([to])
        product = lax.dot_general(
            scaled, o_all[pl.ds(2 * to, 2)].reshape(columns, width),
            (((1,), (1,)), ((), ())), preferred_element_type=f32,
        ).astype(bf16)
        itself = (x == c) & (tp == to)

        @pl.when(itself)
        def _():
            arrived[share] = product
            sq_arrived[share] = sums

        @pl.when(jnp.logical_not(itself))
        def _(to=to, product=product):
            leaving[to] = product
            outward(to).start()
            squares(to).start()

    into.leave()
    for dx, dy in pieces:
        piece(dx, dy).wait_send()
    out_of.leave()
    for to in range(4):
        itself = (x == c) & (x == to // 2) & (y == to % 2)

        @pl.when(jnp.logical_not(itself))
        def _():
            features(to).wait_send()

    @pl.when(jnp.logical_not(last))
    def _():
        edge(after).wait_send()
        for part in range(parts):
            state(part, after).wait_send()

    total, sq_total = 0.0, 0.0
    for slot in range(4):
        @pl.when(jnp.logical_not((x == c) & (share == slot)))
        def _():
            remote(
                leaving.at[0], arrived.at[slot], send.at[0], recv.at[slot], seq, tp + 1 - 2 * c
            ).wait_recv()
            remote(
                sq_leaving, sq_arrived.at[slot], sq_send.at[0], sq_recv.at[slot],
                seq, tp + 1 - 2 * c,
            ).wait_recv()

        total = total + arrived[slot].astype(f32)
        sq_total = sq_total + sq_arrived[slot]
    scale = lax.rsqrt(sq_total[0:1] / inner_total + EPSILON)
    scale_rows = jnp.transpose(jnp.broadcast_to(scale, (128, tokens)))[:, 0:1]
    out_ref[...] = (total * scale_rows).astype(out_ref.dtype)

    for to in range(4):
        itself = (x == c) & (tp == to)

        @pl.when(jnp.logical_not(itself))
        def _():
            outward(to).wait_send()
            squares(to).wait_send()


def on_device_paired(
    hidden_in,
    w_in_gate,
    w_in_value,
    w_in_shared,
    w_in_step,
    conv_value,
    conv_shared,
    dt_bias,
    a_log,
    skip_gain,
    norm_gain,
    w_out,
    prompt_lengths,
    row_blocks,
):
    blocks = lax.axis_size("seq")
    planes = blocks // 2
    tokens, features = hidden_in.shape
    rows, width = w_in_value.shape
    shared_width, heads = w_in_shared.shape[1], dt_bias.shape[0]
    mix_width = width + shared_width // 2
    in_width = mix_width + width
    state_size = shared_width // 2
    out_columns = w_out.shape[1]
    f32, bf16, dma = jnp.float32, jnp.bfloat16, pltpu.SemaphoreType.DMA
    vmem, smem = pl.BlockSpec(memory_space=pltpu.VMEM), pl.BlockSpec(memory_space=pltpu.SMEM)

    def relay_sems(chunks):
        return [dma((blocks, chunks)), dma((chunks,))] + [dma((planes, chunks))] * 3

    arguments = (
        hidden_in,
        w_in_gate,
        w_in_value,
        w_in_shared,
        w_in_step.T,
        conv_value,
        conv_shared,
        dt_bias[None],
        a_log[None],
        skip_gain[None],
        norm_gain[None],
        w_out.T,
    )
    return pl.pallas_call(
        functools.partial(mixer_kernel, planes, heads, width * lax.axis_size("tp")),
        out_shape=jax.ShapeDtypeStruct((tokens, features), bf16),
        in_specs=[smem] * 2 + [pl.BlockSpec(memory_space=pl.ANY)] * len(arguments),
        out_specs=vmem,
        scratch_shapes=[pltpu.VMEM(array.shape, array.dtype) for array in arguments]
        + [
            dma((len(arguments),)),
            pltpu.VMEM((rows, in_width), bf16),
            pltpu.VMEM((blocks, rows, in_width), bf16),
            pltpu.VMEM((out_columns, width), bf16),
            pltpu.VMEM((blocks, out_columns, width), bf16),
            pltpu.VMEM((tokens, in_width), f32),
            pltpu.VMEM((2, tokens, features // 2), bf16),
            pltpu.VMEM((8, tokens, features // 2), bf16),
            pltpu.VMEM((8, width), f32),
            pltpu.VMEM((8, width), f32),
            pltpu.VMEM((tokens, width), bf16),
            pltpu.VMEM((tokens + 8, mix_width), f32),
            pltpu.VMEM((16, mix_width), bf16),
            pltpu.VMEM((16, mix_width), bf16),
            pltpu.VMEM((tokens, width + shared_width), bf16),
            pltpu.VMEM((tokens, shared_width // 2), bf16),
            pltpu.VMEM((4, tokens, shared_width // 2), bf16),
            pltpu.VMEM((width, state_size), f32),
            pltpu.VMEM((width, state_size), bf16),
            pltpu.VMEM((width, state_size), bf16),
            pltpu.VMEM((4, tokens, features), bf16),
            pltpu.VMEM((4, tokens, features), bf16),
            pltpu.VMEM((8, tokens), f32),
            pltpu.VMEM((4, 8, tokens), f32),
        ]
        + relay_sems(rows // 48)
        + relay_sems(out_columns // 96)
        + [dma((4,)), dma((4,)), dma((2,)), dma((2,)), dma((2, 4)), dma((2, 4))]
        + [dma((4,))] * 4,
        compiler_params=pltpu.CompilerParams(
            collective_id=0, has_side_effects=True, vmem_limit_bytes=58 << 20
        ),
        name="mixer",
    )(prompt_lengths, row_blocks, *arguments)


def paired(mesh):
    return dict(mesh.shape) == {"seq": 8, "tp": 4}


def solution(mesh):
    return jax.shard_map(
        on_device_paired if paired(mesh) else on_device_plain,
        mesh=mesh,
        in_specs=(
            P("seq", "tp"),
            P("seq", "tp"),
            P("seq", "tp"),
            P("seq", None),
            P("seq", "tp"),
            P(None, "tp"),
            P(),
            P("tp"),
            P("tp"),
            P("tp"),
            P("tp"),
            P("tp", "seq"),
            P(),
            P(),
        ),
        out_specs=P("seq", "tp"),
        check_vma=False,
    )
```
